32 devices in a mesh: dp: 4 (over x, core), mp: 8 (over z, y).
Axes of the slice: x: 2, y: 2, z: 4, core: 2. Of those that a mesh axis runs over, the one named last changes fastest.
Arguments:
- prompt_rows: bfloat16 [16384, 2048], P(('dp', 'mp')), may hold values from -6 to 6
- step_rows: bfloat16 [16, 2048], P('dp', 'mp'), may hold values from -6 to 6
- attn_gain: float32 [2048], replicated, may hold values from 0.1 to 1.9
- latent_gain: float32 [512], replicated, may hold values from 0.1 to 1.9
- joined_qkva: float32 [2048, 3648], P('dp', 'mp'), may hold values from -2.4748737 to 2.4748737
- kv_up: float32 [512, 4096], P('dp', 'mp'), may hold values from -0.25 to 0.25
- out_proj: float32 [2048, 2048], P('dp', 'mp'), may hold values from -1.5 to 1.5
- latent_cache: bfloat16 [256, 16, 576], P(('dp', 'mp')), may hold values from -6 to 6
- page_table: int32 [16, 8], P('dp'), may hold values from 0 to 63, as said below
- cached_lengths: int32 [16], P('dp'), may hold values from 1 to 127, as said below
Outputs:
- prompt_out: bfloat16 [16384, 2048], P(('dp', 'mp'))
- step_out: bfloat16 [16, 2048], P('dp', 'mp')
The draws below stay inside these ranges and needn't reach their ends.
Inputs may be any that keep to these rules, and one draw needn't show every extreme that they name: `page_table`: row r lists the slots of r's 8 pages, numbered within the pool of r's index of dp; slot g lies on index g // 8 of mp. No slot is listed twice within one index of dp. `cached_lengths`: some request has 127 cached tokens and some has one.
All inputs are finite; a program needn't handle non-finite values.
Results may differ from the reference program's by a relative error of at most 0.015.
Values may be sent and summed in bfloat16 or wider, within the bound.
A program may use at most 128 MiB of HBM per device.

```python
import math
import jax
import jax.numpy as jnp
from jax import lax

D = 2048
H = 16
DN = 128
DR = 64
DV = 128
LAT = 512
LEN = 512
PAGE = 16
CTX = 128
REQ_GRP = 4
JOINED = 3648
UPCOLS = 4096
HEADOUT = 2048
KEYW = 576
PAGES_REQ = 8
GROUP_POOL = 64
TOKENS = 16384
REQS = 16
POOL_ALL = 256
N_DP = 4


def draw_joined_qkva(key, part):
    base_key = jax.random.fold_in(jax.random.fold_in(key, 17), 0)
    base = jax.random.normal(base_key, (D, JOINED), jnp.float32)
    return jnp.clip(base, -6.0, 6.0) * D ** (-0.5)


def draw_page_table(key, part):
    group_count = REQS // REQ_GRP
    taken_count = REQ_GRP * PAGES_REQ

    def one_group(group_key):
        chosen = jax.random.permutation(group_key, GROUP_POOL)[:taken_count]
        chosen = jnp.where(chosen == jnp.max(chosen), GROUP_POOL - 1, chosen)
        chosen = jnp.where(chosen == jnp.min(chosen), 0, chosen)
        return chosen.reshape(REQ_GRP, PAGES_REQ)
    tables = jax.vmap(one_group)(jax.random.split(key, group_count))
    return tables.reshape(REQS, PAGES_REQ).astype(jnp.int32)


def draw_cached_lengths(key, part):
    length_key, place_key = jax.random.split(key)
    lengths = jax.random.randint(length_key, (REQS,), 1, CTX)
    picked = jax.random.permutation(place_key, REQS)
    lengths = lengths.at[picked[0]].set(CTX - 1)
    lengths = lengths.at[picked[1]].set(1)
    return lengths.astype(jnp.int32)


def level_of(rng, extent, cuts, low, high):
    gain, own = 1.0, jax.random.fold_in(rng, 6)
    for axis_at, parts in cuts:
        steps = jnp.exp(jax.random.uniform(jax.random.fold_in(own, axis_at), (parts,), jnp.float32, low / len(cuts), high / len(cuts)))
        gain = gain * jnp.repeat(steps, extent[axis_at] // parts).reshape([-1 if axis == axis_at else 1 for axis in range(len(extent))])
    return gain


def normal_values(rng, dims, width, reach, shards=(), kind=jnp.bfloat16):
    factor_of = level_of(rng, dims, shards, -0.22, 0.18) if shards else 1.0
    entries = jax.random.normal(rng, dims, jnp.float32) * width * factor_of
    return jnp.minimum(jnp.maximum(entries, -reach), reach).astype(kind)


def setup_inputs(seed: int = 0) -> dict:
    keys = jax.random.split(jax.random.key(seed), 11)
    return {
        "prompt_rows": normal_values(keys[0], (TOKENS, D), 1.0, 6.0, ((0, 32),)),
        "step_rows": normal_values(keys[1], (REQS, D), 1.0, 6.0, ((0, 4), (1, 8))),
        "attn_gain": jnp.clip(1.0 + 0.18 * jax.random.normal(keys[2], (D,), jnp.float32), 0.1, 1.9),
        "latent_gain": jnp.clip(1.0 + 0.18 * jax.random.normal(keys[3], (LAT,), jnp.float32), 0.1, 1.9),
        "joined_qkva": draw_joined_qkva(jax.random.fold_in(keys[10], 71), 0),
        "kv_up": normal_values(keys[5], (LAT, UPCOLS), LAT ** -0.5, 0.25, ((0, 4), (1, 8)), jnp.float32),
        "out_proj": normal_values(keys[6], (HEADOUT, D), H ** -0.5, 1.5, ((0, 4), (1, 8)), jnp.float32),
        "latent_cache": normal_values(keys[7], (POOL_ALL, PAGE, KEYW), 1.0, 6.0, ((0, 32),)),
        "page_table": draw_page_table(jax.random.fold_in(keys[10], 71), 0),
        "cached_lengths": draw_cached_lengths(jax.random.fold_in(keys[10], 71), 0),
    }


NORM_EPS = 1e-06
ROPE_BASE = 50000.0
MASKED = -1e+30

def rms_scale(values, scales):
    widened = values.astype(jnp.float32)
    mean_square = lax.optimization_barrier(jnp.mean(widened * widened, axis=-1, keepdims=True))
    return widened * lax.rsqrt(mean_square + NORM_EPS) * scales

def rotate(values, positions):
    rot_width = values.shape[-1]
    half_width = rot_width // 2
    freq_steps = jnp.arange(half_width, dtype=jnp.float32)
    inv_freqs = jnp.exp(freq_steps * (-2.0 * math.log(ROPE_BASE) / rot_width))
    angles = positions.astype(jnp.float32)[:, None] * inv_freqs[None, :]
    angle_shape = (positions.shape[0],) + (1,) * (values.ndim - 2) + (half_width,)
    cosine = jnp.cos(angles).reshape(angle_shape)
    sine_part = jnp.sin(angles).reshape(angle_shape)
    lower_half = values[..., :half_width]
    upper_half = values[..., half_width:]
    return jnp.concatenate([lower_half * cosine - upper_half * sine_part, upper_half * cosine + lower_half * sine_part], axis=-1)

def attend(queries, key_rows, allowed, score_scale):
    scores = jnp.einsum('qhc,kc->qhk', queries.astype(jnp.float32), key_rows.astype(jnp.float32)) * score_scale
    scores = jnp.where(allowed[:, None, :], scores, MASKED)
    peak_score = lax.optimization_barrier(jnp.max(scores, axis=-1, keepdims=True))
    weights = jnp.where(allowed[:, None, :], jnp.exp(scores - peak_score), 0.0)
    weight_sum = lax.optimization_barrier(jnp.sum(weights, axis=-1, keepdims=True))
    half_weights = lax.optimization_barrier(weights.astype(jnp.bfloat16)).astype(jnp.float32)
    summed = jnp.einsum('qhk,kl->qhl', half_weights, key_rows[:, :LAT].astype(jnp.float32))
    return (summed / weight_sum).astype(jnp.bfloat16)

def reference(prompt_rows, step_rows, attn_gain, latent_gain, joined_qkva, kv_up, out_proj, latent_cache, page_table, cached_lengths):
    score_scale = (DN + DR) ** (-0.5)
    w_joined = joined_qkva.astype(jnp.bfloat16)
    w_up = kv_up.astype(jnp.bfloat16)
    w_output = out_proj.astype(jnp.bfloat16)
    up_heads = w_up.reshape(LAT, H, DN + DV)
    head_cols = H * (DN + DR)

    def queries_keys(source_rows, positions):
        normed = rms_scale(source_rows, attn_gain).astype(jnp.bfloat16)
        projected = jnp.dot(normed, w_joined, preferred_element_type=jnp.float32).astype(jnp.bfloat16)
        row_count = projected.shape[0]
        query_cols = projected[:, :head_cols].reshape(row_count, H, DN + DR)
        query_rot = rotate(query_cols[..., DN:].astype(jnp.float32), positions).astype(jnp.bfloat16)
        latent = rms_scale(projected[:, head_cols:head_cols + LAT], latent_gain).astype(jnp.bfloat16)
        key_rot = rotate(projected[:, head_cols + LAT:].astype(jnp.float32), positions).astype(jnp.bfloat16)
        query_lat = jnp.einsum('rhn,lhn->rhl', query_cols[..., :DN].astype(jnp.float32), up_heads[..., :DN].astype(jnp.float32)).astype(jnp.bfloat16)
        queries = jnp.concatenate([query_lat, query_rot], axis=-1)
        key_rows = jnp.concatenate([latent, key_rot], axis=-1)
        return (queries, key_rows)

    def finish(latent_out):
        heads_out = jnp.einsum('rhl,lhv->rhv', latent_out.astype(jnp.float32), up_heads[..., DN:].astype(jnp.float32)).astype(jnp.bfloat16)
        heads_out = heads_out.reshape(latent_out.shape[0], H * DV)
        return jnp.dot(heads_out, w_output, preferred_element_type=jnp.float32).astype(jnp.bfloat16)

    def one_prompt(tokens):
        positions = jnp.arange(LEN, dtype=jnp.int32)
        queries, key_rows = queries_keys(tokens, positions)
        allowed = positions[None, :] <= positions[:, None]
        return finish(attend(queries, key_rows, allowed, score_scale))
    prompt_out = lax.map(one_prompt, prompt_rows.reshape(-1, LEN, D)).reshape(-1, D)
    queries, key_rows = queries_keys(step_rows, cached_lengths)
    cache_groups = latent_cache.reshape(N_DP, GROUP_POOL, PAGE, LAT + DR)
    group_ids = jnp.arange(REQS, dtype=jnp.int32) // REQ_GRP
    pages = cache_groups[group_ids[:, None], page_table].reshape(REQS, CTX, LAT + DR)
    key_all = jnp.concatenate([pages, key_rows[:, None, :]], axis=1)
    cached_ok = jnp.arange(CTX, dtype=jnp.int32)[None, :] < cached_lengths[:, None]
    allowed_all = jnp.concatenate([cached_ok, jnp.ones((REQS, 1), dtype=jnp.bool_)], axis=1)

    def one_request(query_one, key_one, allowed_one):
        return attend(query_one[None], key_one, allowed_one[None], score_scale)[0]
    step_latent = jax.vmap(one_request)(queries, key_all, allowed_all)
    step_out = finish(step_latent)
    return (prompt_out, step_out)
```

```python
import functools
import math

import jax
import jax.numpy as jnp
from jax import lax
from jax.experimental import pallas as pl
from jax.experimental.pallas import tpu as pltpu
from jax.sharding import PartitionSpec as P

H = 16
DN = 128
DR = 64
DV = 128
LAT = 512
LEN = 512


NORM_EPS = 1e-06
ROPE_BASE = 50000.0
MASKED = -1e30


def merged(x, axis, combine):
    everything = jax.tree.map(
        lambda part, kind: lax.all_gather(part.astype(kind), axis),
        x,
        jax.tree.map(lambda a: jnp.bfloat16 if a.dtype == jnp.float32 else a.dtype, x),
    )

    def take(k):
        return jax.tree.map(lambda part, own: part[k].astype(own.dtype), everything, x)

    return lax.fori_loop(
        1, lax.axis_size(axis), lambda k, so_far: combine(so_far, take(k)), take(0)
    )


def rms_scale(values, scales):
    widened = values.astype(jnp.float32)
    mean_square = jnp.mean(widened * widened, axis=-1, keepdims=True)
    return widened * lax.rsqrt(mean_square + NORM_EPS) * scales


def rotate(values, positions):
    rot_width = values.shape[-1]
    half_width = rot_width // 2
    freq_steps = jnp.arange(half_width, dtype=jnp.float32)
    inv_freqs = jnp.exp(freq_steps * (-2.0 * math.log(ROPE_BASE) / rot_width))
    angles = positions.astype(jnp.float32)[:, None] * inv_freqs[None, :]
    angle_shape = (positions.shape[0],) + (1,) * (values.ndim - 2) + (half_width,)
    cosine = jnp.cos(angles).reshape(angle_shape)
    sine_part = jnp.sin(angles).reshape(angle_shape)
    lower_half = values[..., :half_width]
    upper_half = values[..., half_width:]
    return jnp.concatenate(
        [
            lower_half * cosine - upper_half * sine_part,
            upper_half * cosine + lower_half * sine_part,
        ],
        axis=-1,
    )


def queries_keys(projected, positions, latent_gain, up_heads):
    head_cols = H * (DN + DR)
    row_count = projected.shape[0]
    query_cols = projected[:, :head_cols].reshape(row_count, H, DN + DR)
    query_rot = rotate(query_cols[..., DN:].astype(jnp.float32), positions).astype(jnp.bfloat16)
    latent = rms_scale(projected[:, head_cols : head_cols + LAT], latent_gain).astype(jnp.bfloat16)
    key_rot = rotate(projected[:, head_cols + LAT :].astype(jnp.float32), positions).astype(
        jnp.bfloat16
    )
    query_lat = jnp.einsum(
        "rhn,lhn->rhl", query_cols[..., :DN], up_heads[..., :DN], preferred_element_type=jnp.float32
    ).astype(jnp.bfloat16)
    queries = jnp.concatenate([query_lat, query_rot], axis=-1)
    key_rows = jnp.concatenate([latent, key_rot], axis=-1)
    return (queries, key_rows)


def prompt_attention(queries, query_ids, all_keys, all_ids, score_scale):
    row_count = queries.shape[0]
    block_rows = min(row_count, 512)
    block_count = row_count // block_rows
    query_blocks = queries.reshape(block_count, block_rows, H, queries.shape[-1])
    id_blocks = query_ids.reshape(block_count, block_rows)
    latent_keys = all_keys[:, :LAT]

    def one_block(block_args):
        query_part, id_part = block_args
        scores = (
            jnp.einsum("qhc,kc->qhk", query_part, all_keys, preferred_element_type=jnp.float32)
            * score_scale
        )
        same_prompt = id_part[:, None] // LEN == all_ids[None, :] // LEN
        allowed = same_prompt & (all_ids[None, :] <= id_part[:, None])
        scores = jnp.where(allowed[:, None, :], scores, MASKED)
        peak_score = jnp.max(scores, axis=-1, keepdims=True)
        weights = jnp.where(allowed[:, None, :], jnp.exp(scores - peak_score), 0.0)
        weight_sum = jnp.sum(weights, axis=-1, keepdims=True)
        summed = jnp.einsum(
            "qhk,kl->qhl",
            weights.astype(jnp.bfloat16),
            latent_keys,
            preferred_element_type=jnp.float32,
        )
        return (summed / weight_sum).astype(jnp.bfloat16)

    return lax.map(one_block, (query_blocks, id_blocks)).reshape(row_count, H, LAT)


def page_attention(queries, latent_cache, page_table, cached_lengths, mp_index, score_scale):
    slot_count = latent_cache.shape[0]
    page_rows = latent_cache.shape[1]
    flat_cache = latent_cache.reshape(slot_count * page_rows, latent_cache.shape[2])
    slot_ids = mp_index * slot_count + jnp.arange(slot_count, dtype=jnp.int32)
    matches = page_table[:, :, None] == slot_ids[None, None, :]
    owned = jnp.any(matches, axis=1)
    page_numbers = jnp.arange(page_table.shape[1], dtype=jnp.int32)[None, :, None]
    page_index = jnp.sum(jnp.where(matches, page_numbers, 0), axis=1)
    key_position = (
        page_index[:, :, None] * page_rows + jnp.arange(page_rows, dtype=jnp.int32)[None, None, :]
    )
    allowed = owned[:, :, None] & (key_position < cached_lengths[:, None, None])
    allowed = allowed.reshape(page_table.shape[0], slot_count * page_rows)
    scores = (
        jnp.einsum("rhc,kc->rhk", queries, flat_cache, preferred_element_type=jnp.float32)
        * score_scale
    )
    scores = jnp.where(allowed[:, None, :], scores, MASKED)
    peak_score = jnp.max(scores, axis=-1)
    weights = jnp.where(allowed[:, None, :], jnp.exp(scores - peak_score[..., None]), 0.0)
    weight_sum = jnp.sum(weights, axis=-1)
    summed = jnp.einsum(
        "rhk,kl->rhl",
        weights.astype(jnp.bfloat16),
        flat_cache[:, :LAT],
        preferred_element_type=jnp.float32,
    )
    return (peak_score, weight_sum, summed)


def combine_partial(first_state, second_state):
    peak_score = jnp.maximum(first_state[0], second_state[0])
    first_factor = jnp.exp(first_state[0] - peak_score)
    second_factor = jnp.exp(second_state[0] - peak_score)
    weight_sum = first_state[1] * first_factor + second_state[1] * second_factor
    summed = first_state[2] * first_factor[..., None] + second_state[2] * second_factor[..., None]
    return (peak_score, weight_sum, summed)


def on_device(
    prompt_rows,
    step_rows,
    attn_gain,
    latent_gain,
    joined_qkva,
    kv_up,
    out_proj,
    latent_cache,
    page_table,
    cached_lengths,
):
    prompt_count = prompt_rows.shape[0]
    mp_index = lax.axis_index("mp")
    mp_size = lax.axis_size("mp")
    score_scale = (DN + DR) ** (-0.5)
    trainer = (
        joined_qkva.astype(jnp.bfloat16),
        kv_up.astype(jnp.bfloat16),
        out_proj.astype(jnp.bfloat16),
    )
    step_full = lax.all_gather(step_rows, "mp", axis=1, tiled=True)
    stacked = jnp.concatenate([prompt_rows, step_full], axis=0)
    normed = rms_scale(stacked, attn_gain).astype(jnp.bfloat16)
    prompt_ids = jnp.arange(prompt_count, dtype=jnp.int32)
    positions = jnp.concatenate([prompt_ids % LEN, cached_lengths], axis=0)
    served = (
        lax.all_to_all(trainer[0], "mp", split_axis=0, concat_axis=1, tiled=True),
        lax.all_to_all(trainer[1], "mp", split_axis=0, concat_axis=1, tiled=True),
        lax.all_to_all(trainer[2], "mp", split_axis=0, concat_axis=1, tiled=True),
    )
    inputs = normed
    projected = jnp.dot(
        inputs,
        lax.all_gather(served[0], ("dp", "mp"), axis=0, tiled=True),
        preferred_element_type=jnp.float32,
    )
    up_full = lax.all_gather(served[1], ("dp", "mp"), axis=0, tiled=True)
    up_heads = up_full.reshape(LAT, H, DN + DV)
    queries, key_rows = queries_keys(
        projected.astype(jnp.bfloat16), positions, latent_gain, up_heads
    )
    prompt_queries = queries[:prompt_count]
    prompt_key_rows = key_rows[:prompt_count]
    step_queries = queries[prompt_count:]
    step_keys = key_rows[prompt_count:]
    prompt_latent = prompt_attention(
        prompt_queries, prompt_ids, prompt_key_rows, prompt_ids, score_scale
    )
    partial_state = page_attention(
        step_queries, latent_cache, page_table, cached_lengths, mp_index, score_scale
    )
    peak_score, weight_sum, summed = merged(partial_state, "mp", combine_partial)
    own_score = (
        jnp.einsum("rhc,rc->rh", step_queries, step_keys, preferred_element_type=jnp.float32)
        * score_scale
    )
    new_peak = jnp.maximum(peak_score, own_score)
    old_factor = jnp.exp(peak_score - new_peak)
    own_weight = jnp.exp(own_score - new_peak)
    weight_sum = weight_sum * old_factor + own_weight
    own_latent = step_keys[:, :LAT].astype(jnp.float32)
    own_half = own_weight.astype(jnp.bfloat16).astype(jnp.float32)
    summed = summed * old_factor[..., None] + own_half[..., None] * own_latent[:, None, :]
    step_latent = (summed / weight_sum[..., None]).astype(jnp.bfloat16)
    latent_out = jnp.concatenate([prompt_latent, step_latent], axis=0)
    heads_out = jnp.einsum(
        "rhl,lhv->rhv", latent_out, up_heads[..., DN:], preferred_element_type=jnp.float32
    ).astype(jnp.bfloat16)
    heads_out = heads_out.reshape(latent_out.shape[0], H * DV)
    inputs = heads_out
    attended = jnp.dot(
        inputs,
        lax.all_gather(served[2], ("dp", "mp"), axis=0, tiled=True),
        preferred_element_type=jnp.float32,
    )
    attended = attended.astype(jnp.bfloat16)
    prompt_out = attended[:prompt_count]
    col_width = attended.shape[1] // mp_size
    step_out = lax.dynamic_slice_in_dim(attended[prompt_count:], mp_index * col_width, col_width, 1)
    return (prompt_out, step_out)


MESH = pl.DeviceIdType.MESH
STEP_LANES = 128
STEP_ROWS = 16
NN = (((1,), (0,)), ((), ()))
NT = (((1,), (1,)), ((), ()))


def mxu(a, b, dims=NN):
    return lax.dot_general(a, b, dims, preferred_element_type=jnp.float32)


def fused_kernel(
    sizes,
    x_ref,
    step_ref,
    gain_ref,
    lat_gain_ref,
    joined_ref,
    up_ref,
    out_w_ref,
    cache_ref,
    cos_ref,
    sin_ref,
    bias_ref,
    out_ref,
    step_out_ref,
    jbuf,
    ubuf,
    obuf,
    sbuf,
    cbuf,
    normed,
    proj,
    lat_t,
    keys,
    q_steps,
    heads,
    send_sem,
    recv_sem,
    small_send,
    small_recv,
):
    rows, dp_size, mp_size, block_cols, z_size = sizes
    dp = lax.axis_index("dp")
    mp = lax.axis_index("mp")
    x, core = dp // 2, dp % 2
    z, y = mp // 2, mp % 2
    bufs = (jbuf, ubuf, obuf)
    pad_cols = jbuf.shape[1]
    j_cut = (pad_cols // 32) * 16 + (16 if (pad_cols // 16) % 2 else 0)
    cuts = ((0, j_cut, pad_cols), (0, 64, 128), (0, 256, 512))
    d_model = normed.shape[1]
    depth = d_model // dp_size

    def dev(xx, cc, yy, zz):
        return (xx * 2 + cc, zz * 2 + yy)

    def slot_of(xx, cc, yy, zz):
        return (xx * 2 + cc) * mp_size + zz * 2 + yy

    me = slot_of(x, core, y, z)
    y_dev = dev(x, core, 1 - y, z)
    x_dev = dev(1 - x, core, y, z)
    core_dev = dev(x, 1 - core, y, z)

    def z_of(j):
        return lax.rem(z + 1 + j, z_size)

    barrier = pltpu.get_barrier_semaphore()
    friends = [dev(x, core, y, z_of(j)) for j in range(z_size - 1)] + [y_dev, x_dev, core_dev]
    for friend in friends:
        pl.semaphore_signal(barrier, inc=1, device_id=friend, device_id_type=MESH)

    def copy(t, hf, slot, index, target):
        lo, hi = cuts[t][hf], cuts[t][hf + 1]
        ref = bufs[t].at[slot, pl.ds(lo, hi - lo)]
        return pltpu.make_async_remote_copy(
            src_ref=ref,
            dst_ref=ref,
            send_sem=send_sem.at[t, hf, index],
            recv_sem=recv_sem.at[t, hf, slot],
            device_id=target,
            device_id_type=MESH,
        )

    def arrived(t, hf, slot):
        copy(t, hf, slot, 0, core_dev).wait_recv()

    axis_devs = ((y_dev, x_dev), (x_dev, y_dev))

    def begin(t):
        for hf in range(2):
            for j in range(z_size - 1):
                copy(t, hf, me, j, dev(x, core, y, z_of(j))).start()
            copy(t, hf, me, 3, axis_devs[hf][0]).start()
            copy(t, hf, me, 7, axis_devs[hf][1]).start()
            copy(t, hf, me, 15, core_dev).start()

    def near(hf, zz, first, second):
        if hf == 0:
            return slot_of(second, core, first, zz)
        return slot_of(first, core, second, zz)

    def event(t, e):
        @pl.when(e < 3)
        def _():
            for hf in range(2):
                slot = slot_of(x, core, y, z_of(e))
                arrived(t, hf, slot)
                copy(t, hf, slot, 4 + e, axis_devs[hf][0]).start()
                copy(t, hf, slot, 8 + e, axis_devs[hf][1]).start()
                copy(t, hf, slot, 16 + e, core_dev).start()

        @pl.when((e >= 3) & (e < 7))
        def _():
            j = e - 3
            zz = lax.rem(z + j, z_size)
            for hf in range(2):
                slot = near(hf, zz, 1 - (y, x)[hf], (x, y)[hf])
                arrived(t, hf, slot)
                copy(t, hf, slot, 11 + j, axis_devs[hf][1]).start()
                copy(t, hf, slot, 19 + j, core_dev).start()

        @pl.when((e >= 7) & (e < 15))
        def _():
            j = e - 7
            zz = lax.rem(z + j, z_size)
            for hf in range(2):
                first = lax.rem((y, x)[hf] + j // z_size, 2)
                slot = near(hf, zz, first, 1 - (x, y)[hf])
                arrived(t, hf, slot)
                copy(t, hf, slot, 23 + j, core_dev).start()

    def small(k, slot, index, target):
        ref = (sbuf, cbuf)[k].at[slot]
        return pltpu.make_async_remote_copy(
            src_ref=ref,
            dst_ref=ref,
            send_sem=small_send.at[k, index],
            recv_sem=small_recv.at[k, slot],
            device_id=target,
            device_id_type=MESH,
        )

    def small_begin(k):
        for j in range(z_size - 1):
            small(k, mp, j, dev(x, core, y, z_of(j))).start()
        small(k, mp, 3, y_dev).start()

    def small_forward(k):
        for j in range(z_size - 1):
            slot = z_of(j) * 2 + y
            small(k, slot, 0, y_dev).wait_recv()
            small(k, slot, 4 + j, y_dev).start()

    def small_finish(k):
        for j in range(z_size):
            slot = lax.rem(z + j, z_size) * 2 + 1 - y
            small(k, slot, 0, y_dev).wait_recv()

    jbuf[me] = joined_ref[...]
    sbuf[mp] = step_ref[...]
    pl.semaphore_wait(barrier, len(friends))
    small_begin(0)
    begin(0)

    for hh in range(2):
        base = hh * (DN + DV)
        ubuf[me, :, base : base + DN] = up_ref[:, base : base + DN].astype(jnp.bfloat16)
        ubuf[me, :, base + DN : base + DN + DV] = (
            up_ref[:, base + DN : base + DN + DV].T.astype(jnp.bfloat16)
        )
    obuf[me] = out_w_ref[...].astype(jnp.bfloat16)
    cbuf[mp] = cache_ref[...]
    small_forward(0)

    @pl.loop(0, rows // 64)
    def _(i):
        at = pl.ds(pl.multiple_of(i * 64, 64), 64)
        normed[at, :] = rms_scale(x_ref[at, :], gain_ref[...]).astype(jnp.bfloat16)

    small_finish(0)
    step_full = jnp.concatenate([sbuf[m] for m in range(mp_size)], axis=1)
    normed[rows : rows + STEP_ROWS, :] = rms_scale(step_full, gain_ref[...]).astype(jnp.bfloat16)
    normed[rows + STEP_ROWS :, :] = jnp.zeros(
        (STEP_LANES - STEP_ROWS, d_model), jnp.bfloat16
    )

    @pl.loop(0, 7)
    def _(e):
        event(0, e)

    begin(1)
    small_begin(1)

    @pl.loop(7, 15)
    def _(e):
        event(0, e)

    small_forward(1)

    def sibling_arrived(t, m):
        for xx in range(2):
            for hf in range(2):
                arrived(t, hf, (xx * 2 + 1 - core) * mp_size + m)

    @pl.loop(0, mp_size)
    def _(m):
        sibling_arrived(0, m)
        event(1, 2 * m)

        @pl.when(m == 2)
        def _():
            begin(2)

        total = mxu(jbuf[m], normed[:, :depth], NT)
        for d in range(1, dp_size):
            total += mxu(jbuf[d * mp_size + m], normed[:, d * depth : (d + 1) * depth], NT)
        proj[pl.ds(pl.multiple_of(m * block_cols, 8), block_cols), :] = total[:block_cols]
        event(1, 2 * m + 1)

    head_cols = H * (DN + DR)
    latent = proj[head_cols : head_cols + LAT, :].astype(jnp.bfloat16).astype(jnp.float32)
    mean_square = jnp.mean(latent * latent, axis=0, keepdims=True)
    latent = latent * lax.rsqrt(mean_square + NORM_EPS) * lat_gain_ref[...]
    lat_t[...] = latent.astype(jnp.bfloat16)

    def turned(part):
        part = part.astype(jnp.bfloat16).astype(jnp.float32)
        low, high = part[: DR // 2], part[DR // 2 :]
        cosine, sine = cos_ref[...], sin_ref[...]
        return jnp.concatenate(
            [low * cosine - high * sine, high * cosine + low * sine], axis=0
        )

    keys[:, :LAT] = latent.T.astype(jnp.bfloat16)
    keys[:, LAT:] = turned(proj[head_cols + LAT : head_cols + LAT + DR, :]).T.astype(jnp.bfloat16)
    q_steps[...] = jnp.zeros_like(q_steps)
    scale2 = (DN + DR) ** (-0.5) * math.log2(math.e)
    half = rows // 2
    causal = lax.broadcasted_iota(jnp.int32, (half, half), 0) <= lax.broadcasted_iota(
        jnp.int32, (half, half), 1
    )

    def attend(scores, values):
        peak = jnp.max(scores, axis=0, keepdims=True)
        weights = jnp.exp2((scores - peak) * scale2)
        weight_sum = jnp.sum(weights, axis=0, keepdims=True)
        summed = mxu(values, weights.astype(jnp.bfloat16))
        return (summed / weight_sum).astype(jnp.bfloat16)

    def uk_uv(m, hh):
        base = hh * (DN + DV)
        w_uk = jnp.concatenate(
            [ubuf[d * mp_size + m, :, base : base + DN] for d in range(dp_size)], axis=0
        )
        w_uv_t = jnp.concatenate(
            [ubuf[d * mp_size + m, :, base + DN : base + DN + DV] for d in range(dp_size)], axis=1
        )
        return w_uk, w_uv_t

    @pl.loop(0, mp_size)
    def _(m):
        sibling_arrived(1, m)
        for hh in range(2):
            event(2, 2 * m + hh)
            first = pl.multiple_of(m * 2 * (DN + DR), 2 * (DN + DR)) + hh * (DN + DR)
            first = pl.multiple_of(first, 64)
            w_uk, w_uv_t = uk_uv(m, hh)
            nope = proj[pl.ds(first, DN), :].astype(jnp.bfloat16)
            q_rot = turned(proj[pl.ds(first + DN, DR), :]).astype(jnp.bfloat16)
            q_lat = mxu(w_uk, nope).astype(jnp.bfloat16)
            query = jnp.concatenate([q_lat, q_rot], axis=0)
            q_steps[...] += pltpu.roll(
                query[:, rows:].astype(jnp.float32), m * 8 + hh * 4, axis=1
            )
            scores = mxu(keys[:half, :], query[:, :half])
            low = attend(jnp.where(causal, scores, MASKED), lat_t[:, :half])
            top = mxu(keys[:half, :], query[:, half:rows])
            end = mxu(keys[half:rows, :], query[:, half:rows])
            scores = jnp.concatenate([top, jnp.where(causal, end, MASKED)], axis=0)
            high = attend(scores, lat_t[:, :rows])
            column = pl.ds(pl.multiple_of(m * 2 * DV + hh * DV, DV), DV)
            heads[:half, column] = mxu(w_uv_t, low).T.astype(jnp.bfloat16)
            heads[half:rows, column] = mxu(w_uv_t, high).T.astype(jnp.bfloat16)

    small_finish(1)
    own_keys = keys[rows : rows + STEP_ROWS, :]
    all_keys = jnp.concatenate([cbuf[m] for m in range(mp_size)] + [own_keys], axis=0)
    scores = mxu(q_steps[...].T.astype(jnp.bfloat16), all_keys, NT) + bias_ref[...]
    peak = jnp.max(scores, axis=1, keepdims=True)
    weights = jnp.exp2((scores - peak) * scale2)
    weight_sum = jnp.sum(weights, axis=1, keepdims=True)
    summed = mxu(weights.astype(jnp.bfloat16), all_keys[:, :LAT])
    step_latent = (summed / weight_sum).astype(jnp.bfloat16)
    heads[rows:, :] = jnp.zeros((STEP_ROWS, H * DV), jnp.bfloat16)
    for h in range(H):
        _, w_uv_t = uk_uv(h // 2, h % 2)
        part = mxu(step_latent, w_uv_t, NT)
        padded = jnp.concatenate(
            [part[4 * h : 4 * h + 4], jnp.zeros((STEP_ROWS - 4, DV), jnp.float32)], axis=0
        )
        heads[rows:, h * DV : (h + 1) * DV] = padded.astype(jnp.bfloat16)

    @pl.loop(0, mp_size)
    def _(m):
        sibling_arrived(2, m)
        total = mxu(heads[:, :depth], obuf[m])
        for d in range(1, dp_size):
            total += mxu(heads[:, d * depth : (d + 1) * depth], obuf[d * mp_size + m])
        width = total.shape[1]
        done = total.astype(jnp.bfloat16)
        out_ref[:, pl.ds(pl.multiple_of(m * width, width), width)] = done[:rows]

        @pl.when(m == mp)
        def _():
            step_out_ref[...] = done[rows:]

    for t in range(3):
        for hf in range(2):

            @pl.loop(0, 31)
            def _(i):
                copy(t, hf, me, i, core_dev).wait_send()

    for k in range(2):

        @pl.loop(0, 7)
        def _(i):
            small(k, mp, i, y_dev).wait_send()


def fused_device(
    prompt_rows,
    step_rows,
    attn_gain,
    latent_gain,
    joined_qkva,
    kv_up,
    out_proj,
    latent_cache,
    page_table,
    cached_lengths,
):
    rows, d_model = prompt_rows.shape
    dp_size, mp_size = lax.axis_size("dp"), lax.axis_size("mp")
    block_cols = joined_qkva.shape[1]
    pad_cols = -(-block_cols // 16) * 16
    joined_t = jnp.pad(joined_qkva.T.astype(jnp.bfloat16), ((0, pad_cols - block_cols), (0, 0)))
    requests = step_rows.shape[0]
    steps = jnp.pad(step_rows, ((0, STEP_ROWS - requests), (0, 0)))
    slot_count, page_rows, key_width = latent_cache.shape
    lanes = rows + STEP_LANES

    positions = jnp.concatenate(
        [
            jnp.arange(rows, dtype=jnp.int32),
            cached_lengths,
            jnp.zeros((STEP_LANES - requests,), jnp.int32),
        ]
    )
    freq_steps = jnp.arange(DR // 2, dtype=jnp.float32)
    inv_freqs = jnp.exp(freq_steps * (-2.0 * math.log(ROPE_BASE) / DR))
    angles = inv_freqs[:, None] * positions.astype(jnp.float32)[None, :]

    matches = page_table[:, :, None] == jnp.arange(slot_count * mp_size, dtype=jnp.int32)
    owned = jnp.any(matches, axis=1)
    page_numbers = jnp.arange(page_table.shape[1], dtype=jnp.int32)[None, :, None]
    page_index = jnp.sum(jnp.where(matches, page_numbers, 0), axis=1)
    key_position = page_index[:, :, None] * page_rows + jnp.arange(page_rows, dtype=jnp.int32)
    allowed = owned[:, :, None] & (key_position < cached_lengths[:, None, None])
    allowed = jnp.concatenate(
        [allowed.reshape(requests, -1), jnp.eye(requests, STEP_ROWS, dtype=jnp.bool_)], axis=1
    )
    bias = jnp.where(allowed, 0.0, MASKED).astype(jnp.float32)
    bias = jnp.tile(bias, (STEP_LANES // requests, 1))

    sizes = (rows, dp_size, mp_size, block_cols, mp_size // 2)
    devices = dp_size * mp_size
    bf16, f32 = jnp.bfloat16, jnp.float32
    vmem = pl.BlockSpec(memory_space=pltpu.VMEM)
    prompt_out, step_out = pl.pallas_call(
        functools.partial(fused_kernel, sizes),
        out_shape=(
            jax.ShapeDtypeStruct((rows, d_model), bf16),
            jax.ShapeDtypeStruct((STEP_ROWS, out_proj.shape[1]), bf16),
        ),
        in_specs=[vmem] * 11,
        out_specs=(vmem, vmem),
        scratch_shapes=[
            pltpu.VMEM((devices, pad_cols, joined_qkva.shape[0]), bf16),
            pltpu.VMEM((devices,) + kv_up.shape, bf16),
            pltpu.VMEM((devices,) + out_proj.shape, bf16),
            pltpu.VMEM((mp_size, STEP_ROWS, step_rows.shape[1]), bf16),
            pltpu.VMEM((mp_size, slot_count * page_rows, key_width), bf16),
            pltpu.VMEM((lanes, d_model), bf16),
            pltpu.VMEM((mp_size * block_cols, lanes), f32),
            pltpu.VMEM((LAT, lanes), bf16),
            pltpu.VMEM((lanes, LAT + DR), bf16),
            pltpu.VMEM((LAT + DR, STEP_LANES), f32),
            pltpu.VMEM((rows + STEP_ROWS, H * DV), bf16),
            pltpu.SemaphoreType.DMA((3, 2, 31)),
            pltpu.SemaphoreType.DMA((3, 2, devices)),
            pltpu.SemaphoreType.DMA((2, 7)),
            pltpu.SemaphoreType.DMA((2, mp_size)),
        ],
        compiler_params=pltpu.CompilerParams(
            collective_id=0, has_side_effects=True, vmem_limit_bytes=64 * 1024 * 1024
        ),
    )(
        prompt_rows,
        steps,
        attn_gain[None, :],
        latent_gain[:, None],
        joined_t,
        kv_up,
        out_proj,
        latent_cache.reshape(slot_count * page_rows, key_width),
        jnp.cos(angles),
        jnp.sin(angles),
        bias,
    )
    return prompt_out, step_out[:requests]


def solution(mesh):
    placed = (
        P(("dp", "mp"), None),
        P("dp", "mp"),
        P(),
        P(),
        P("dp", "mp"),
        P("dp", "mp"),
        P("dp", "mp"),
        P(("dp", "mp"), None, None),
        P("dp", None),
        P("dp"),
    )
    fits = mesh.shape["dp"] == 4 and mesh.shape["mp"] == 8
    return jax.shard_map(
        fused_device if fits else on_device,
        mesh=mesh,
        in_specs=placed,
        out_specs=(P(("dp", "mp"), None), P("dp", "mp")),
        check_vma=False,
    )
```

```python
import functools
import math

import jax
import jax.numpy as jnp
from jax import lax
from jax.experimental import pallas as pl
from jax.experimental.pallas import tpu as pltpu
from jax.sharding import PartitionSpec as P

H = 16
DN = 128
DR = 64
DV = 128
LAT = 512
LEN = 512


NORM_EPS = 1e-06
ROPE_BASE = 50000.0
MASKED = -1e30


def merged(x, axis, combine):
    everything = jax.tree.map(
        lambda part, kind: lax.all_gather(part.astype(kind), axis),
        x,
        jax.tree.map(lambda a: jnp.bfloat16 if a.dtype == jnp.float32 else a.dtype, x),
    )

    def take(k):
        return jax.tree.map(lambda part, own: part[k].astype(own.dtype), everything, x)

    return lax.fori_loop(
        1, lax.axis_size(axis), lambda k, so_far: combine(so_far, take(k)), take(0)
    )


def rms_scale(values, scales):
    widened = values.astype(jnp.float32)
    mean_square = jnp.mean(widened * widened, axis=-1, keepdims=True)
    return widened * lax.rsqrt(mean_square + NORM_EPS) * scales


def rotate(values, positions):
    rot_width = values.shape[-1]
    half_width = rot_width // 2
    freq_steps = jnp.arange(half_width, dtype=jnp.float32)
    inv_freqs = jnp.exp(freq_steps * (-2.0 * math.log(ROPE_BASE) / rot_width))
    angles = positions.astype(jnp.float32)[:, None] * inv_freqs[None, :]
    angle_shape = (positions.shape[0],) + (1,) * (values.ndim - 2) + (half_width,)
    cosine = jnp.cos(angles).reshape(angle_shape)
    sine_part = jnp.sin(angles).reshape(angle_shape)
    lower_half = values[..., :half_width]
    upper_half = values[..., half_width:]
    return jnp.concatenate(
        [
            lower_half * cosine - upper_half * sine_part,
            upper_half * cosine + lower_half * sine_part,
        ],
        axis=-1,
    )


def queries_keys(projected, positions, latent_gain, up_heads):
    head_cols = H * (DN + DR)
    row_count = projected.shape[0]
    query_cols = projected[:, :head_cols].reshape(row_count, H, DN + DR)
    query_rot = rotate(query_cols[..., DN:].astype(jnp.float32), positions).astype(jnp.bfloat16)
    latent = rms_scale(projected[:, head_cols : head_cols + LAT], latent_gain).astype(jnp.bfloat16)
    key_rot = rotate(projected[:, head_cols + LAT :].astype(jnp.float32), positions).astype(
        jnp.bfloat16
    )
    query_lat = jnp.einsum(
        "rhn,lhn->rhl", query_cols[..., :DN], up_heads[..., :DN], preferred_element_type=jnp.float32
    ).astype(jnp.bfloat16)
    queries = jnp.concatenate([query_lat, query_rot], axis=-1)
    key_rows = jnp.concatenate([latent, key_rot], axis=-1)
    return (queries, key_rows)


def prompt_attention(queries, query_ids, all_keys, all_ids, score_scale):
    row_count = queries.shape[0]
    block_rows = min(row_count, 512)
    block_count = row_count // block_rows
    query_blocks = queries.reshape(block_count, block_rows, H, queries.shape[-1])
    id_blocks = query_ids.reshape(block_count, block_rows)
    latent_keys = all_keys[:, :LAT]

    def one_block(block_args):
        query_part, id_part = block_args
        scores = (
            jnp.einsum("qhc,kc->qhk", query_part, all_keys, preferred_element_type=jnp.float32)
            * score_scale
        )
        same_prompt = id_part[:, None] // LEN == all_ids[None, :] // LEN
        allowed = same_prompt & (all_ids[None, :] <= id_part[:, None])
        scores = jnp.where(allowed[:, None, :], scores, MASKED)
        peak_score = jnp.max(scores, axis=-1, keepdims=True)
        weights = jnp.where(allowed[:, None, :], jnp.exp(scores - peak_score), 0.0)
        weight_sum = jnp.sum(weights, axis=-1, keepdims=True)
        summed = jnp.einsum(
            "qhk,kl->qhl",
            weights.astype(jnp.bfloat16),
            latent_keys,
            preferred_element_type=jnp.float32,
        )
        return (summed / weight_sum).astype(jnp.bfloat16)

    return lax.map(one_block, (query_blocks, id_blocks)).reshape(row_count, H, LAT)


def page_attention(queries, latent_cache, page_table, cached_lengths, mp_index, score_scale):
    slot_count = latent_cache.shape[0]
    page_rows = latent_cache.shape[1]
    flat_cache = latent_cache.reshape(slot_count * page_rows, latent_cache.shape[2])
    slot_ids = mp_index * slot_count + jnp.arange(slot_count, dtype=jnp.int32)
    matches = page_table[:, :, None] == slot_ids[None, None, :]
    owned = jnp.any(matches, axis=1)
    page_numbers = jnp.arange(page_table.shape[1], dtype=jnp.int32)[None, :, None]
    page_index = jnp.sum(jnp.where(matches, page_numbers, 0), axis=1)
    key_position = (
        page_index[:, :, None] * page_rows + jnp.arange(page_rows, dtype=jnp.int32)[None, None, :]
    )
    allowed = owned[:, :, None] & (key_position < cached_lengths[:, None, None])
    allowed = allowed.reshape(page_table.shape[0], slot_count * page_rows)
    scores = (
        jnp.einsum("rhc,kc->rhk", queries, flat_cache, preferred_element_type=jnp.float32)
        * score_scale
    )
    scores = jnp.where(allowed[:, None, :], scores, MASKED)
    peak_score = jnp.max(scores, axis=-1)
    weights = jnp.where(allowed[:, None, :], jnp.exp(scores - peak_score[..., None]), 0.0)
    weight_sum = jnp.sum(weights, axis=-1)
    summed = jnp.einsum(
        "rhk,kl->rhl",
        weights.astype(jnp.bfloat16),
        flat_cache[:, :LAT],
        preferred_element_type=jnp.float32,
    )
    return (peak_score, weight_sum, summed)


def combine_partial(first_state, second_state):
    peak_score = jnp.maximum(first_state[0], second_state[0])
    first_factor = jnp.exp(first_state[0] - peak_score)
    second_factor = jnp.exp(second_state[0] - peak_score)
    weight_sum = first_state[1] * first_factor + second_state[1] * second_factor
    summed = first_state[2] * first_factor[..., None] + second_state[2] * second_factor[..., None]
    return (peak_score, weight_sum, summed)


def on_device(
    prompt_rows,
    step_rows,
    attn_gain,
    latent_gain,
    joined_qkva,
    kv_up,
    out_proj,
    latent_cache,
    page_table,
    cached_lengths,
):
    prompt_count = prompt_rows.shape[0]
    mp_index = lax.axis_index("mp")
    mp_size = lax.axis_size("mp")
    score_scale = (DN + DR) ** (-0.5)
    trainer = (
        joined_qkva.astype(jnp.bfloat16),
        kv_up.astype(jnp.bfloat16),
        out_proj.astype(jnp.bfloat16),
    )
    step_full = lax.all_gather(step_rows, "mp", axis=1, tiled=True)
    stacked = jnp.concatenate([prompt_rows, step_full], axis=0)
    normed = rms_scale(stacked, attn_gain).astype(jnp.bfloat16)
    prompt_ids = jnp.arange(prompt_count, dtype=jnp.int32)
    positions = jnp.concatenate([prompt_ids % LEN, cached_lengths], axis=0)
    served = (
        lax.all_to_all(trainer[0], "mp", split_axis=0, concat_axis=1, tiled=True),
        lax.all_to_all(trainer[1], "mp", split_axis=0, concat_axis=1, tiled=True),
        lax.all_to_all(trainer[2], "mp", split_axis=0, concat_axis=1, tiled=True),
    )
    inputs = normed
    projected = jnp.dot(
        inputs,
        lax.all_gather(served[0], ("dp", "mp"), axis=0, tiled=True),
        preferred_element_type=jnp.float32,
    )
    up_full = lax.all_gather(served[1], ("dp", "mp"), axis=0, tiled=True)
    up_heads = up_full.reshape(LAT, H, DN + DV)
    queries, key_rows = queries_keys(
        projected.astype(jnp.bfloat16), positions, latent_gain, up_heads
    )
    prompt_queries = queries[:prompt_count]
    prompt_key_rows = key_rows[:prompt_count]
    step_queries = queries[prompt_count:]
    step_keys = key_rows[prompt_count:]
    prompt_latent = prompt_attention(
        prompt_queries, prompt_ids, prompt_key_rows, prompt_ids, score_scale
    )
    partial_state = page_attention(
        step_queries, latent_cache, page_table, cached_lengths, mp_index, score_scale
    )
    peak_score, weight_sum, summed = merged(partial_state, "mp", combine_partial)
    own_score = (
        jnp.einsum("rhc,rc->rh", step_queries, step_keys, preferred_element_type=jnp.float32)
        * score_scale
    )
    new_peak = jnp.maximum(peak_score, own_score)
    old_factor = jnp.exp(peak_score - new_peak)
    own_weight = jnp.exp(own_score - new_peak)
    weight_sum = weight_sum * old_factor + own_weight
    own_latent = step_keys[:, :LAT].astype(jnp.float32)
    own_half = own_weight.astype(jnp.bfloat16).astype(jnp.float32)
    summed = summed * old_factor[..., None] + own_half[..., None] * own_latent[:, None, :]
    step_latent = (summed / weight_sum[..., None]).astype(jnp.bfloat16)
    latent_out = jnp.concatenate([prompt_latent, step_latent], axis=0)
    heads_out = jnp.einsum(
        "rhl,lhv->rhv", latent_out, up_heads[..., DN:], preferred_element_type=jnp.float32
    ).astype(jnp.bfloat16)
    heads_out = heads_out.reshape(latent_out.shape[0], H * DV)
    inputs = heads_out
    attended = jnp.dot(
        inputs,
        lax.all_gather(served[2], ("dp", "mp"), axis=0, tiled=True),
        preferred_element_type=jnp.float32,
    )
    attended = attended.astype(jnp.bfloat16)
    prompt_out = attended[:prompt_count]
    col_width = attended.shape[1] // mp_size
    step_out = lax.dynamic_slice_in_dim(attended[prompt_count:], mp_index * col_width, col_width, 1)
    return (prompt_out, step_out)


MESH = pl.DeviceIdType.MESH
STEP_LANES = 128
STEP_ROWS = 16
NN = (((1,), (0,)), ((), ()))
NT = (((1,), (1,)), ((), ()))


def mxu(a, b, dims=NN):
    return lax.dot_general(a, b, dims, preferred_element_type=jnp.float32)


def fused_kernel(
    sizes,
    x_ref,
    step_ref,
    gain_ref,
    lat_gain_ref,
    joined_ref,
    up_ref,
    out_w_ref,
    cache_ref,
    table_ref,
    lengths_ref,
    out_ref,
    step_out_ref,
    jbuf,
    ubuf,
    obuf,
    sbuf,
    cbuf,
    normed,
    proj,
    lat_t,
    keys,
    q_steps,
    heads,
    cosine_s,
    sine_s,
    send_sem,
    recv_sem,
    small_send,
    small_recv,
):
    rows, dp_size, mp_size, block_cols, z_size, page_rows = sizes
    dp = lax.axis_index("dp")
    mp = lax.axis_index("mp")
    x, core = dp // 2, dp % 2
    z, y = mp // 2, mp % 2
    bufs = (jbuf, ubuf, obuf)
    pad_cols = jbuf.shape[1]
    cuts = tuple(
        (0, (buf.shape[1] * 59 // 1600) * 16, buf.shape[1]) for buf in bufs
    )
    depth = normed.shape[2]
    requests = step_ref.shape[0]
    lanes = rows + STEP_LANES

    def dev(xx, cc, yy, zz):
        return (xx * 2 + cc, zz * 2 + yy)

    def slot_of(xx, cc, yy, zz):
        return (xx * 2 + cc) * mp_size + zz * 2 + yy

    me = slot_of(x, core, y, z)
    y_dev = dev(x, core, 1 - y, z)
    x_dev = dev(1 - x, core, y, z)
    core_dev = dev(x, 1 - core, y, z)

    def z_of(j):
        return lax.rem(z + 1 + j, z_size)

    barrier = pltpu.get_barrier_semaphore()
    friends = [dev(x, core, y, z_of(j)) for j in range(z_size - 1)] + [y_dev, x_dev, core_dev]
    for friend in friends:
        pl.semaphore_signal(barrier, inc=1, device_id=friend, device_id_type=MESH)

    def copy(t, hf, slot, index, target):
        lo, hi = cuts[t][hf], cuts[t][hf + 1]
        ref = bufs[t].at[slot, pl.ds(lo, hi - lo)]
        return pltpu.make_async_remote_copy(
            src_ref=ref,
            dst_ref=ref,
            send_sem=send_sem.at[t, hf, index],
            recv_sem=recv_sem.at[t, hf, slot],
            device_id=target,
            device_id_type=MESH,
        )

    def arrived(t, hf, slot):
        copy(t, hf, slot, 0, core_dev).wait_recv()

    axis_devs = ((y_dev, x_dev), (x_dev, y_dev))

    def begin(t):
        for hf in range(2):
            for j in range(z_size - 1):
                copy(t, hf, me, j, dev(x, core, y, z_of(j))).start()
            copy(t, hf, me, 3, axis_devs[hf][0]).start()
            copy(t, hf, me, 7, axis_devs[hf][1]).start()
            copy(t, hf, me, 15, core_dev).start()

    def near(hf, zz, first, second):
        if hf == 0:
            return slot_of(second, core, first, zz)
        return slot_of(first, core, second, zz)

    def event(t, e):
        @pl.when(e < 3)
        def _():
            for hf in range(2):
                slot = slot_of(x, core, y, z_of(e))
                arrived(t, hf, slot)
                copy(t, hf, slot, 4 + e, axis_devs[hf][0]).start()
                copy(t, hf, slot, 8 + e, axis_devs[hf][1]).start()
                copy(t, hf, slot, 16 + e, core_dev).start()

        @pl.when((e >= 3) & (e < 7))
        def _():
            j = e - 3
            zz = lax.rem(z + j, z_size)
            for hf in range(2):
                slot = near(hf, zz, 1 - (y, x)[hf], (x, y)[hf])
                arrived(t, hf, slot)
                copy(t, hf, slot, 11 + j, axis_devs[hf][1]).start()
                copy(t, hf, slot, 19 + j, core_dev).start()

        @pl.when((e >= 7) & (e < 15))
        def _():
            j = e - 7
            zz = lax.rem(z + j, z_size)
            for hf in range(2):
                first = lax.rem((y, x)[hf] + j // z_size, 2)
                slot = near(hf, zz, first, 1 - (x, y)[hf])
                arrived(t, hf, slot)
                copy(t, hf, slot, 23 + j, core_dev).start()

    def small(k, slot, index, target):
        ref = (sbuf, cbuf)[k].at[slot]
        return pltpu.make_async_remote_copy(
            src_ref=ref,
            dst_ref=ref,
            send_sem=small_send.at[k, index],
            recv_sem=small_recv.at[k, slot],
            device_id=target,
            device_id_type=MESH,
        )

    def small_begin(k):
        for j in range(z_size - 1):
            small(k, mp, j, dev(x, core, y, z_of(j))).start()
        small(k, mp, 3, y_dev).start()

    def small_forward(k):
        for j in range(z_size - 1):
            slot = z_of(j) * 2 + y
            small(k, slot, 0, y_dev).wait_recv()
            small(k, slot, 4 + j, y_dev).start()

    def small_finish(k):
        for j in range(z_size):
            slot = lax.rem(z + j, z_size) * 2 + 1 - y
            small(k, slot, 0, y_dev).wait_recv()

    whole_cols = block_cols // 128 * 128
    rest_cols = block_cols - whole_cols
    jbuf[me, :whole_cols, :] = joined_ref[:, :whole_cols].T.astype(jnp.bfloat16)
    rest = jnp.concatenate(
        [joined_ref[:, whole_cols:], jnp.zeros((depth, 128 - rest_cols), jnp.float32)], axis=1
    )
    jbuf[me, whole_cols:, :] = rest.T[: pad_cols - whole_cols].astype(jnp.bfloat16)
    sbuf[mp] = jnp.concatenate(
        [
            step_ref[...].astype(jnp.float32),
            jnp.zeros((STEP_ROWS - requests, step_ref.shape[1]), jnp.float32),
        ],
        axis=0,
    ).astype(jnp.bfloat16)
    pl.semaphore_wait(barrier, len(friends))
    small_begin(0)
    begin(0)

    for hh in range(2):
        base = hh * (DN + DV)
        ubuf[me, :, base : base + DN] = up_ref[:, base : base + DN].astype(jnp.bfloat16)
        ubuf[me, :, base + DN : base + DN + DV] = (
            up_ref[:, base + DN : base + DN + DV].T.astype(jnp.bfloat16)
        )
    obuf[me] = out_w_ref[...].astype(jnp.bfloat16)
    cbuf[mp] = cache_ref[...]
    small_forward(0)

    @pl.loop(0, rows // 64)
    def _(i):
        at = pl.ds(pl.multiple_of(i * 64, 64), 64)
        part = rms_scale(x_ref[at, :], gain_ref[...]).astype(jnp.bfloat16)
        for d in range(dp_size):
            normed[d, at, :] = part[:, d * depth : (d + 1) * depth]

    @pl.loop(0, proj.shape[0] // 64)
    def _(i):
        proj[pl.ds(pl.multiple_of(i * 64, 64), 64), :] = jnp.zeros((64, lanes), jnp.float32)

    small_finish(0)
    step_full = jnp.concatenate([sbuf[m] for m in range(mp_size)], axis=1)
    part = rms_scale(step_full, gain_ref[...]).astype(jnp.bfloat16)
    for d in range(dp_size):
        normed[d, rows : rows + STEP_ROWS, :] = part[:, d * depth : (d + 1) * depth]
        normed[d, rows + STEP_ROWS :, :] = jnp.zeros((STEP_LANES - STEP_ROWS, depth), jnp.bfloat16)

    def slot_at(hf, n, cc):
        zz = lax.rem(z + n, z_size)
        first = lax.rem((y, x)[hf] + n // 4, 2)
        second = lax.rem((x, y)[hf] + n // 8, 2)
        if hf == 0:
            return slot_of(second, cc, first, zz)
        return slot_of(first, cc, second, zz)

    def project(n, cc, wait):
        for hf in range(2):
            slot = slot_at(hf, n, cc)
            if wait:
                arrived(0, hf, slot)
            lo, hi = cuts[0][hf], cuts[0][hf + 1]
            valid = min(hi, block_cols) - lo
            total = mxu(jbuf[slot, lo:hi, :], normed[slot // mp_size], NT)
            at = pl.ds(pl.multiple_of(lax.rem(slot, mp_size) * block_cols + lo, 8), valid)
            proj[at, :] += total[:valid]

    project(0, core, False)

    @pl.loop(1, 16)
    def _(n):
        event(0, n - 1)

        @pl.when(n == 7)
        def _():
            begin(1)
            small_begin(1)

        @pl.when(n >= 12)
        def _():
            event(1, n - 12)

        project(n, core, False)
        project(n - 1, 1 - core, True)

    begin(2)
    small_forward(1)
    project(15, 1 - core, True)

    def sibling_arrived(t, m):
        for xx in range(2):
            for hf in range(2):
                arrived(t, hf, (xx * 2 + 1 - core) * mp_size + m)

    lane = lax.broadcasted_iota(jnp.int32, (DR // 2, lanes), 1)
    positions = jnp.where(lane < rows, lane, 0)
    for r in range(requests):
        positions = jnp.where(lane == rows + r, lengths_ref[r], positions)
    step = lax.broadcasted_iota(jnp.int32, (DR // 2, lanes), 0).astype(jnp.float32)
    angles = positions.astype(jnp.float32) * jnp.exp(step * (-2.0 * math.log(ROPE_BASE) / DR))
    cosine_s[...] = jnp.cos(angles)
    sine_s[...] = jnp.sin(angles)

    head_cols = H * (DN + DR)
    latent = proj[head_cols : head_cols + LAT, :].astype(jnp.bfloat16).astype(jnp.float32)
    mean_square = jnp.mean(latent * latent, axis=0, keepdims=True)
    lat_gain = jnp.broadcast_to(lat_gain_ref[...], (8, LAT)).T[:, :1]
    latent = latent * lax.rsqrt(mean_square + NORM_EPS) * lat_gain
    lat_t[...] = latent.astype(jnp.bfloat16)

    def turned(part):
        part = part.astype(jnp.bfloat16).astype(jnp.float32)
        low, high = part[: DR // 2], part[DR // 2 :]
        cosine, sine = cosine_s[...], sine_s[...]
        return jnp.concatenate(
            [low * cosine - high * sine, high * cosine + low * sine], axis=0
        )

    keys[:, :LAT] = latent.T.astype(jnp.bfloat16)
    keys[:, LAT:] = turned(proj[head_cols + LAT : head_cols + LAT + DR, :]).T.astype(jnp.bfloat16)
    q_steps[...] = jnp.zeros_like(q_steps)
    scale2 = (DN + DR) ** (-0.5) * math.log2(math.e)
    half = rows // 2
    causal = lax.broadcasted_iota(jnp.int32, (half, half), 0) <= lax.broadcasted_iota(
        jnp.int32, (half, half), 1
    )

    def attend(scores, values):
        peak = jnp.max(scores, axis=0, keepdims=True)
        weights = jnp.exp2((scores - peak) * scale2)
        weight_sum = jnp.sum(weights, axis=0, keepdims=True)
        summed = mxu(values, weights.astype(jnp.bfloat16))
        return (summed / weight_sum).astype(jnp.bfloat16)

    def uk_uv(m, hh):
        base = hh * (DN + DV)
        w_uk = jnp.concatenate(
            [ubuf[d * mp_size + m, :, base : base + DN] for d in range(dp_size)], axis=0
        )
        w_uv_t = jnp.concatenate(
            [ubuf[d * mp_size + m, :, base + DN : base + DN + DV] for d in range(dp_size)], axis=1
        )
        return w_uk, w_uv_t

    @pl.loop(4, 15)
    def _(e):
        event(1, e)

        @pl.when(e >= 11)
        def _():
            event(2, e - 11)

    @pl.loop(0, mp_size)
    def _(m):
        sibling_arrived(1, m)
        for hh in range(2):
            event(2, 4 + 2 * m + hh)
            first = pl.multiple_of(m * 2 * (DN + DR), 2 * (DN + DR)) + hh * (DN + DR)
            first = pl.multiple_of(first, 64)
            w_uk, w_uv_t = uk_uv(m, hh)
            nope = proj[pl.ds(first, DN), :].astype(jnp.bfloat16)
            q_rot = turned(proj[pl.ds(first + DN, DR), :]).astype(jnp.bfloat16)
            q_lat = mxu(w_uk, nope).astype(jnp.bfloat16)
            query = jnp.concatenate([q_lat, q_rot], axis=0)
            q_steps[...] += pltpu.roll(
                query[:, rows:].astype(jnp.float32), m * 8 + hh * 4, axis=1
            )
            scores = mxu(keys[:half, :], query[:, :half])
            low = attend(jnp.where(causal, scores, MASKED), lat_t[:, :half])
            top = mxu(keys[:half, :], query[:, half:rows])
            end = mxu(keys[half:rows, :], query[:, half:rows])
            scores = jnp.concatenate([top, jnp.where(causal, end, MASKED)], axis=0)
            high = attend(scores, lat_t[:, :rows])
            column = pl.ds(pl.multiple_of(m * 2 * DV + hh * DV, DV), DV)
            heads[:half, column] = mxu(w_uv_t, low).T.astype(jnp.bfloat16)
            heads[half:rows, column] = mxu(w_uv_t, high).T.astype(jnp.bfloat16)

    small_finish(1)
    own_keys = keys[rows : rows + STEP_ROWS, :]
    all_keys = jnp.concatenate([cbuf[m] for m in range(mp_size)] + [own_keys], axis=0)
    cached = mp_size * cache_ref.shape[0]
    column = lax.broadcasted_iota(jnp.int32, (8, cached), 1)
    request = lax.rem(lax.broadcasted_iota(jnp.int32, (8, cached), 0), requests)
    slot, entry = column // page_rows, lax.rem(column, page_rows)
    bias = jnp.full((8, cached), MASKED, jnp.float32)
    for r in range(requests):
        for page in range(table_ref.shape[1]):
            counts = (slot == table_ref[r, page]) & (page * page_rows + entry < lengths_ref[r])
            bias = jnp.where(counts & (request == r), 0.0, bias)
    own = lax.broadcasted_iota(jnp.int32, (8, STEP_ROWS), 1) == lax.rem(
        lax.broadcasted_iota(jnp.int32, (8, STEP_ROWS), 0), requests
    )
    bias = jnp.concatenate([bias, jnp.where(own, 0.0, MASKED)], axis=1)
    bias = jnp.concatenate([bias] * (STEP_LANES // 8), axis=0)
    scores = mxu(q_steps[...].T.astype(jnp.bfloat16), all_keys, NT) + bias
    peak = jnp.max(scores, axis=1, keepdims=True)
    weights = jnp.exp2((scores - peak) * scale2)
    weight_sum = jnp.sum(weights, axis=1, keepdims=True)
    summed = mxu(weights.astype(jnp.bfloat16), all_keys[:, :LAT])
    step_latent = (summed / weight_sum).astype(jnp.bfloat16)
    heads[rows:, :] = jnp.zeros((STEP_ROWS, H * DV), jnp.bfloat16)
    for h in range(H):
        _, w_uv_t = uk_uv(h // 2, h % 2)
        part = mxu(step_latent, w_uv_t, NT)
        padded = jnp.concatenate(
            [part[4 * h : 4 * h + 4], jnp.zeros((STEP_ROWS - 4, DV), jnp.float32)], axis=0
        )
        heads[rows:, h * DV : (h + 1) * DV] = padded.astype(jnp.bfloat16)

    @pl.loop(0, mp_size)
    def _(m):
        sibling_arrived(2, m)
        total = mxu(heads[:, :depth], obuf[m])
        for d in range(1, dp_size):
            total += mxu(heads[:, d * depth : (d + 1) * depth], obuf[d * mp_size + m])
        width = total.shape[1]
        done = total.astype(jnp.bfloat16)
        out_ref[:, pl.ds(pl.multiple_of(m * width, width), width)] = done[:rows]

        @pl.when(m == mp)
        def _():
            step_out_ref[...] = total[rows : rows + requests].astype(jnp.bfloat16)

    for t in range(3):
        for hf in range(2):

            @pl.loop(0, 31)
            def _(i):
                copy(t, hf, me, i, core_dev).wait_send()

    for k in range(2):

        @pl.loop(0, 7)
        def _(i):
            small(k, mp, i, y_dev).wait_send()


def fused_device(
    prompt_rows,
    step_rows,
    attn_gain,
    latent_gain,
    joined_qkva,
    kv_up,
    out_proj,
    latent_cache,
    page_table,
    cached_lengths,
):
    rows, d_model = prompt_rows.shape
    dp_size, mp_size = lax.axis_size("dp"), lax.axis_size("mp")
    block_cols = joined_qkva.shape[1]
    pad_cols = -(-block_cols // 16) * 16
    requests = step_rows.shape[0]
    slot_count, page_rows, key_width = latent_cache.shape
    lanes = rows + STEP_LANES
    sizes = (rows, dp_size, mp_size, block_cols, mp_size // 2, page_rows)
    devices = dp_size * mp_size
    bf16, f32 = jnp.bfloat16, jnp.float32
    vmem = pl.BlockSpec(memory_space=pltpu.VMEM)
    prompt_out, step_out = pl.pallas_call(
        functools.partial(fused_kernel, sizes),
        out_shape=(
            jax.ShapeDtypeStruct((rows, d_model), bf16),
            jax.ShapeDtypeStruct((requests, out_proj.shape[1]), bf16),
        ),
        in_specs=[vmem] * 8 + [pl.BlockSpec(memory_space=pltpu.SMEM)] * 2,
        out_specs=(vmem, vmem),
        scratch_shapes=[
            pltpu.VMEM((devices, pad_cols, joined_qkva.shape[0]), bf16),
            pltpu.VMEM((devices,) + kv_up.shape, bf16),
            pltpu.VMEM((devices,) + out_proj.shape, bf16),
            pltpu.VMEM((mp_size, STEP_ROWS, step_rows.shape[1]), bf16),
            pltpu.VMEM((mp_size, slot_count * page_rows, key_width), bf16),
            pltpu.VMEM((dp_size, lanes, joined_qkva.shape[0]), bf16),
            pltpu.VMEM((mp_size * block_cols, lanes), f32),
            pltpu.VMEM((LAT, lanes), bf16),
            pltpu.VMEM((lanes, LAT + DR), bf16),
            pltpu.VMEM((LAT + DR, STEP_LANES), f32),
            pltpu.VMEM((rows + STEP_ROWS, H * DV), bf16),
            pltpu.VMEM((DR // 2, lanes), f32),
            pltpu.VMEM((DR // 2, lanes), f32),
            pltpu.SemaphoreType.DMA((3, 2, 31)),
            pltpu.SemaphoreType.DMA((3, 2, devices)),
            pltpu.SemaphoreType.DMA((2, 7)),
            pltpu.SemaphoreType.DMA((2, mp_size)),
        ],
        compiler_params=pltpu.CompilerParams(
            collective_id=0, has_side_effects=True, vmem_limit_bytes=64 * 1024 * 1024
        ),
    )(
        prompt_rows,
        step_rows,
        attn_gain[None, :],
        latent_gain[None, :],
        joined_qkva,
        kv_up,
        out_proj,
        latent_cache.reshape(slot_count * page_rows, key_width),
        page_table,
        cached_lengths,
    )
    return prompt_out, step_out


def solution(mesh):
    placed = (
        P(("dp", "mp"), None),
        P("dp", "mp"),
        P(),
        P(),
        P("dp", "mp"),
        P("dp", "mp"),
        P("dp", "mp"),
        P(("dp", "mp"), None, None),
        P("dp", None),
        P("dp"),
    )
    fits = mesh.shape["dp"] == 4 and mesh.shape["mp"] == 8
    return jax.shard_map(
        fused_device if fits else on_device,
        mesh=mesh,
        in_specs=placed,
        out_specs=(P(("dp", "mp"), None), P("dp", "mp")),
        check_vma=False,
    )
```

```python
import functools
import math

import jax
import jax.numpy as jnp
from jax import lax
from jax.experimental import pallas as pl
from jax.experimental.pallas import tpu as pltpu
from jax.sharding import PartitionSpec as P

H = 16
DN = 128
DR = 64
DV = 128
LAT = 512
LEN = 512


NORM_EPS = 1e-06
ROPE_BASE = 50000.0
MASKED = -1e30


def merged(x, axis, combine):
    everything = jax.tree.map(
        lambda part, kind: lax.all_gather(part.astype(kind), axis),
        x,
        jax.tree.map(lambda a: jnp.bfloat16 if a.dtype == jnp.float32 else a.dtype, x),
    )

    def take(k):
        return jax.tree.map(lambda part, own: part[k].astype(own.dtype), everything, x)

    return lax.fori_loop(
        1, lax.axis_size(axis), lambda k, so_far: combine(so_far, take(k)), take(0)
    )


def rms_scale(values, scales):
    widened = values.astype(jnp.float32)
    mean_square = jnp.mean(widened * widened, axis=-1, keepdims=True)
    return widened * lax.rsqrt(mean_square + NORM_EPS) * scales


def rotate(values, positions):
    rot_width = values.shape[-1]
    half_width = rot_width // 2
    freq_steps = jnp.arange(half_width, dtype=jnp.float32)
    inv_freqs = jnp.exp(freq_steps * (-2.0 * math.log(ROPE_BASE) / rot_width))
    angles = positions.astype(jnp.float32)[:, None] * inv_freqs[None, :]
    angle_shape = (positions.shape[0],) + (1,) * (values.ndim - 2) + (half_width,)
    cosine = jnp.cos(angles).reshape(angle_shape)
    sine_part = jnp.sin(angles).reshape(angle_shape)
    lower_half = values[..., :half_width]
    upper_half = values[..., half_width:]
    return jnp.concatenate(
        [
            lower_half * cosine - upper_half * sine_part,
            upper_half * cosine + lower_half * sine_part,
        ],
        axis=-1,
    )


def queries_keys(projected, positions, latent_gain, up_heads):
    head_cols = H * (DN + DR)
    row_count = projected.shape[0]
    query_cols = projected[:, :head_cols].reshape(row_count, H, DN + DR)
    query_rot = rotate(query_cols[..., DN:].astype(jnp.float32), positions).astype(jnp.bfloat16)
    latent = rms_scale(projected[:, head_cols : head_cols + LAT], latent_gain).astype(jnp.bfloat16)
    key_rot = rotate(projected[:, head_cols + LAT :].astype(jnp.float32), positions).astype(
        jnp.bfloat16
    )
    query_lat = jnp.einsum(
        "rhn,lhn->rhl", query_cols[..., :DN], up_heads[..., :DN], preferred_element_type=jnp.float32
    ).astype(jnp.bfloat16)
    queries = jnp.concatenate([query_lat, query_rot], axis=-1)
    key_rows = jnp.concatenate([latent, key_rot], axis=-1)
    return (queries, key_rows)


def prompt_attention(queries, query_ids, all_keys, all_ids, score_scale):
    row_count = queries.shape[0]
    block_rows = min(row_count, 512)
    block_count = row_count // block_rows
    query_blocks = queries.reshape(block_count, block_rows, H, queries.shape[-1])
    id_blocks = query_ids.reshape(block_count, block_rows)
    latent_keys = all_keys[:, :LAT]

    def one_block(block_args):
        query_part, id_part = block_args
        scores = (
            jnp.einsum("qhc,kc->qhk", query_part, all_keys, preferred_element_type=jnp.float32)
            * score_scale
        )
        same_prompt = id_part[:, None] // LEN == all_ids[None, :] // LEN
        allowed = same_prompt & (all_ids[None, :] <= id_part[:, None])
        scores = jnp.where(allowed[:, None, :], scores, MASKED)
        peak_score = jnp.max(scores, axis=-1, keepdims=True)
        weights = jnp.where(allowed[:, None, :], jnp.exp(scores - peak_score), 0.0)
        weight_sum = jnp.sum(weights, axis=-1, keepdims=True)
        summed = jnp.einsum(
            "qhk,kl->qhl",
            weights.astype(jnp.bfloat16),
            latent_keys,
            preferred_element_type=jnp.float32,
        )
        return (summed / weight_sum).astype(jnp.bfloat16)

    return lax.map(one_block, (query_blocks, id_blocks)).reshape(row_count, H, LAT)


def page_attention(queries, latent_cache, page_table, cached_lengths, mp_index, score_scale):
    slot_count = latent_cache.shape[0]
    page_rows = latent_cache.shape[1]
    flat_cache = latent_cache.reshape(slot_count * page_rows, latent_cache.shape[2])
    slot_ids = mp_index * slot_count + jnp.arange(slot_count, dtype=jnp.int32)
    matches = page_table[:, :, None] == slot_ids[None, None, :]
    owned = jnp.any(matches, axis=1)
    page_numbers = jnp.arange(page_table.shape[1], dtype=jnp.int32)[None, :, None]
    page_index = jnp.sum(jnp.where(matches, page_numbers, 0), axis=1)
    key_position = (
        page_index[:, :, None] * page_rows + jnp.arange(page_rows, dtype=jnp.int32)[None, None, :]
    )
    allowed = owned[:, :, None] & (key_position < cached_lengths[:, None, None])
    allowed = allowed.reshape(page_table.shape[0], slot_count * page_rows)
    scores = (
        jnp.einsum("rhc,kc->rhk", queries, flat_cache, preferred_element_type=jnp.float32)
        * score_scale
    )
    scores = jnp.where(allowed[:, None, :], scores, MASKED)
    peak_score = jnp.max(scores, axis=-1)
    weights = jnp.where(allowed[:, None, :], jnp.exp(scores - peak_score[..., None]), 0.0)
    weight_sum = jnp.sum(weights, axis=-1)
    summed = jnp.einsum(
        "rhk,kl->rhl",
        weights.astype(jnp.bfloat16),
        flat_cache[:, :LAT],
        preferred_element_type=jnp.float32,
    )
    return (peak_score, weight_sum, summed)


def combine_partial(first_state, second_state):
    peak_score = jnp.maximum(first_state[0], second_state[0])
    first_factor = jnp.exp(first_state[0] - peak_score)
    second_factor = jnp.exp(second_state[0] - peak_score)
    weight_sum = first_state[1] * first_factor + second_state[1] * second_factor
    summed = first_state[2] * first_factor[..., None] + second_state[2] * second_factor[..., None]
    return (peak_score, weight_sum, summed)


def on_device(
    prompt_rows,
    step_rows,
    attn_gain,
    latent_gain,
    joined_qkva,
    kv_up,
    out_proj,
    latent_cache,
    page_table,
    cached_lengths,
):
    prompt_count = prompt_rows.shape[0]
    mp_index = lax.axis_index("mp")
    mp_size = lax.axis_size("mp")
    score_scale = (DN + DR) ** (-0.5)
    trainer = (
        joined_qkva.astype(jnp.bfloat16),
        kv_up.astype(jnp.bfloat16),
        out_proj.astype(jnp.bfloat16),
    )
    step_full = lax.all_gather(step_rows, "mp", axis=1, tiled=True)
    stacked = jnp.concatenate([prompt_rows, step_full], axis=0)
    normed = rms_scale(stacked, attn_gain).astype(jnp.bfloat16)
    prompt_ids = jnp.arange(prompt_count, dtype=jnp.int32)
    positions = jnp.concatenate([prompt_ids % LEN, cached_lengths], axis=0)
    served = (
        lax.all_to_all(trainer[0], "mp", split_axis=0, concat_axis=1, tiled=True),
        lax.all_to_all(trainer[1], "mp", split_axis=0, concat_axis=1, tiled=True),
        lax.all_to_all(trainer[2], "mp", split_axis=0, concat_axis=1, tiled=True),
    )
    inputs = normed
    projected = jnp.dot(
        inputs,
        lax.all_gather(served[0], ("dp", "mp"), axis=0, tiled=True),
        preferred_element_type=jnp.float32,
    )
    up_full = lax.all_gather(served[1], ("dp", "mp"), axis=0, tiled=True)
    up_heads = up_full.reshape(LAT, H, DN + DV)
    queries, key_rows = queries_keys(
        projected.astype(jnp.bfloat16), positions, latent_gain, up_heads
    )
    prompt_queries = queries[:prompt_count]
    prompt_key_rows = key_rows[:prompt_count]
    step_queries = queries[prompt_count:]
    step_keys = key_rows[prompt_count:]
    prompt_latent = prompt_attention(
        prompt_queries, prompt_ids, prompt_key_rows, prompt_ids, score_scale
    )
    partial_state = page_attention(
        step_queries, latent_cache, page_table, cached_lengths, mp_index, score_scale
    )
    peak_score, weight_sum, summed = merged(partial_state, "mp", combine_partial)
    own_score = (
        jnp.einsum("rhc,rc->rh", step_queries, step_keys, preferred_element_type=jnp.float32)
        * score_scale
    )
    new_peak = jnp.maximum(peak_score, own_score)
    old_factor = jnp.exp(peak_score - new_peak)
    own_weight = jnp.exp(own_score - new_peak)
    weight_sum = weight_sum * old_factor + own_weight
    own_latent = step_keys[:, :LAT].astype(jnp.float32)
    own_half = own_weight.astype(jnp.bfloat16).astype(jnp.float32)
    summed = summed * old_factor[..., None] + own_half[..., None] * own_latent[:, None, :]
    step_latent = (summed / weight_sum[..., None]).astype(jnp.bfloat16)
    latent_out = jnp.concatenate([prompt_latent, step_latent], axis=0)
    heads_out = jnp.einsum(
        "rhl,lhv->rhv", latent_out, up_heads[..., DN:], preferred_element_type=jnp.float32
    ).astype(jnp.bfloat16)
    heads_out = heads_out.reshape(latent_out.shape[0], H * DV)
    inputs = heads_out
    attended = jnp.dot(
        inputs,
        lax.all_gather(served[2], ("dp", "mp"), axis=0, tiled=True),
        preferred_element_type=jnp.float32,
    )
    attended = attended.astype(jnp.bfloat16)
    prompt_out = attended[:prompt_count]
    col_width = attended.shape[1] // mp_size
    step_out = lax.dynamic_slice_in_dim(attended[prompt_count:], mp_index * col_width, col_width, 1)
    return (prompt_out, step_out)


MESH = pl.DeviceIdType.MESH
STEP_LANES = 128
STEP_ROWS = 16
NN = (((1,), (0,)), ((), ()))
NT = (((1,), (1,)), ((), ()))


def mxu(a, b, dims=NN):
    return lax.dot_general(a, b, dims, preferred_element_type=jnp.float32)


def fused_kernel(
    sizes,
    x_ref,
    step_ref,
    gain_ref,
    lat_gain_ref,
    joined_ref,
    up_ref,
    out_w_ref,
    cache_ref,
    table_ref,
    lengths_ref,
    out_ref,
    step_out_ref,
    jbuf,
    ubuf,
    obuf,
    sbuf,
    cbuf,
    normed,
    proj,
    lat_t,
    keys,
    q_steps,
    heads,
    cosine_s,
    sine_s,
    send_sem,
    recv_sem,
    small_send,
    small_recv,
):
    rows, dp_size, mp_size, block_cols, z_size, page_rows = sizes
    dp = lax.axis_index("dp")
    mp = lax.axis_index("mp")
    x, core = dp // 2, dp % 2
    z, y = mp // 2, mp % 2
    bufs = (jbuf, ubuf, obuf)
    pad_cols = jbuf.shape[1]
    cuts = tuple(
        (0, (buf.shape[1] * 59 // 1600) * 16, buf.shape[1]) for buf in bufs
    )
    depth = normed.shape[2]
    requests = step_ref.shape[0]
    lanes = rows + STEP_LANES

    def dev(xx, cc, yy, zz):
        return (xx * 2 + cc, zz * 2 + yy)

    def slot_of(xx, cc, yy, zz):
        return (xx * 2 + cc) * mp_size + zz * 2 + yy

    me = slot_of(x, core, y, z)
    y_dev = dev(x, core, 1 - y, z)
    x_dev = dev(1 - x, core, y, z)
    core_dev = dev(x, 1 - core, y, z)

    middle = (z == 1) | (z == 2)

    def z_at(n):
        far = z // 2
        inner = lax.rem(lax.rem(z + 1, z_size) // 2, 2)
        place = (1 - inner) * n + inner * (lax.rem(n + 1, 3) + n // 3 * 2)
        return (1 - far) * place + far * (z_size - 1 - place)

    def z_next(e):
        odd = lax.rem(e, 2)
        return dev(x, core, y, (1 - odd) * 3 * (z - 1) + odd * (3 - z))

    def z_neighbours(act):
        @pl.when(z > 0)
        def _():
            act(0, dev(x, core, y, z - 1))

        @pl.when(z < z_size - 1)
        def _():
            act(1, dev(x, core, y, z + 1))

    barrier = pltpu.get_barrier_semaphore()

    def greet(_, friend):
        pl.semaphore_signal(barrier, inc=1, device_id=friend, device_id_type=MESH)

    z_neighbours(greet)
    for friend in (y_dev, x_dev, core_dev):
        greet(None, friend)

    def copy(t, hf, slot, index, target):
        lo, hi = cuts[t][hf], cuts[t][hf + 1]
        ref = bufs[t].at[slot, pl.ds(lo, hi - lo)]
        return pltpu.make_async_remote_copy(
            src_ref=ref,
            dst_ref=ref,
            send_sem=send_sem.at[t, hf, index],
            recv_sem=recv_sem.at[t, hf, slot],
            device_id=target,
            device_id_type=MESH,
        )

    def arrived(t, hf, slot):
        copy(t, hf, slot, 0, core_dev).wait_recv()

    axis_devs = ((y_dev, x_dev), (x_dev, y_dev))

    def begin(t):
        for hf in range(2):
            z_neighbours(lambda i, target: copy(t, hf, me, i, target).start())
            copy(t, hf, me, 3, axis_devs[hf][0]).start()
            copy(t, hf, me, 7, axis_devs[hf][1]).start()
            copy(t, hf, me, 15, core_dev).start()

    def near(hf, zz, first, second):
        if hf == 0:
            return slot_of(second, core, first, zz)
        return slot_of(first, core, second, zz)

    def event(t, e):
        @pl.when(e < 3)
        def _():
            for hf in range(2):
                slot = slot_of(x, core, y, z_at(e + 1))
                arrived(t, hf, slot)

                @pl.when(middle)
                def _():
                    copy(t, hf, slot, 31 + e, z_next(e)).start()

                copy(t, hf, slot, 4 + e, axis_devs[hf][0]).start()
                copy(t, hf, slot, 8 + e, axis_devs[hf][1]).start()
                copy(t, hf, slot, 16 + e, core_dev).start()

        @pl.when((e >= 3) & (e < 7))
        def _():
            j = e - 3
            zz = z_at(j)
            for hf in range(2):
                slot = near(hf, zz, 1 - (y, x)[hf], (x, y)[hf])
                arrived(t, hf, slot)
                copy(t, hf, slot, 11 + j, axis_devs[hf][1]).start()
                copy(t, hf, slot, 19 + j, core_dev).start()

        @pl.when((e >= 7) & (e < 15))
        def _():
            j = e - 7
            zz = z_at(lax.rem(j, z_size))
            for hf in range(2):
                first = lax.rem((y, x)[hf] + j // z_size, 2)
                slot = near(hf, zz, first, 1 - (x, y)[hf])
                arrived(t, hf, slot)
                copy(t, hf, slot, 23 + j, core_dev).start()

    def small(k, slot, index, target):
        ref = (sbuf, cbuf)[k].at[slot]
        return pltpu.make_async_remote_copy(
            src_ref=ref,
            dst_ref=ref,
            send_sem=small_send.at[k, index],
            recv_sem=small_recv.at[k, slot],
            device_id=target,
            device_id_type=MESH,
        )

    def small_begin(k):
        z_neighbours(lambda i, target: small(k, mp, i, target).start())
        small(k, mp, 2, y_dev).start()

    def small_forward(k):
        for e in range(z_size - 1):
            slot = z_at(e + 1) * 2 + y
            small(k, slot, 0, y_dev).wait_recv()

            @pl.when(middle)
            def _():
                small(k, slot, 6 + e, z_next(e)).start()

            small(k, slot, 3 + e, y_dev).start()

    def small_finish(k):
        for j in range(z_size):
            slot = z_at(j) * 2 + 1 - y
            small(k, slot, 0, y_dev).wait_recv()

    jbuf[me] = jnp.concatenate(
        [joined_ref[...], jnp.zeros((pad_cols - block_cols, depth), jnp.float32)], axis=0
    ).astype(jnp.bfloat16)
    sbuf[mp] = jnp.concatenate(
        [
            step_ref[...].astype(jnp.float32),
            jnp.zeros((STEP_ROWS - requests, step_ref.shape[1]), jnp.float32),
        ],
        axis=0,
    ).astype(jnp.bfloat16)
    pl.semaphore_wait(barrier, 4 + lax.rem((z + 1) // 2, 2))
    small_begin(0)
    begin(0)

    for hh in range(2):
        base = hh * (DN + DV)
        ubuf[me, :, base : base + DN] = up_ref[:, base : base + DN].astype(jnp.bfloat16)
        ubuf[me, :, base + DN : base + DN + DV] = (
            up_ref[:, base + DN : base + DN + DV].T.astype(jnp.bfloat16)
        )
    obuf[me] = out_w_ref[...].astype(jnp.bfloat16)
    cbuf[mp] = cache_ref[...]
    small_forward(0)

    @pl.loop(0, rows // 64)
    def _(i):
        at = pl.ds(pl.multiple_of(i * 64, 64), 64)
        part = rms_scale(x_ref[at, :], gain_ref[...]).astype(jnp.bfloat16)
        for d in range(dp_size):
            normed[d, at, :] = part[:, d * depth : (d + 1) * depth]

    @pl.loop(0, proj.shape[0] // 64)
    def _(i):
        proj[pl.ds(pl.multiple_of(i * 64, 64), 64), :] = jnp.zeros((64, lanes), jnp.float32)

    small_finish(0)
    step_full = jnp.concatenate([sbuf[m] for m in range(mp_size)], axis=1)
    part = rms_scale(step_full, gain_ref[...]).astype(jnp.bfloat16)
    for d in range(dp_size):
        normed[d, rows : rows + STEP_ROWS, :] = part[:, d * depth : (d + 1) * depth]
        normed[d, rows + STEP_ROWS :, :] = jnp.zeros((STEP_LANES - STEP_ROWS, depth), jnp.bfloat16)

    def slot_at(hf, n, cc):
        zz = z_at(n % 4)
        first = lax.rem((y, x)[hf] + n // 4, 2)
        second = lax.rem((x, y)[hf] + n // 8, 2)
        if hf == 0:
            return slot_of(second, cc, first, zz)
        return slot_of(first, cc, second, zz)

    def project(n, cc, wait):
        for hf in range(2):
            slot = slot_at(hf, n, cc)
            if wait:
                arrived(0, hf, slot)
            lo, hi = cuts[0][hf], cuts[0][hf + 1]
            valid = min(hi, block_cols) - lo
            total = mxu(jbuf[slot, lo:hi, :], normed[slot // mp_size], NT)
            at = pl.ds(pl.multiple_of(lax.rem(slot, mp_size) * block_cols + lo, 8), valid)
            proj[at, :] += total[:valid]

    project(0, core, False)

    @pl.loop(1, 16)
    def _(n):
        event(0, n - 1)

        @pl.when(n == 7)
        def _():
            begin(1)
            small_begin(1)

        @pl.when(n >= 12)
        def _():
            event(1, n - 12)

        project(n, core, False)
        project(n - 1, 1 - core, True)

    begin(2)
    small_forward(1)
    project(15, 1 - core, True)

    def sibling_arrived(t, m):
        for xx in range(2):
            for hf in range(2):
                arrived(t, hf, (xx * 2 + 1 - core) * mp_size + m)

    lane = lax.broadcasted_iota(jnp.int32, (DR // 2, lanes), 1)
    positions = jnp.where(lane < rows, lane, 0)
    for r in range(requests):
        positions = jnp.where(lane == rows + r, lengths_ref[r], positions)
    step = lax.broadcasted_iota(jnp.int32, (DR // 2, lanes), 0).astype(jnp.float32)
    angles = positions.astype(jnp.float32) * jnp.exp(step * (-2.0 * math.log(ROPE_BASE) / DR))
    cosine_s[...] = jnp.cos(angles)
    sine_s[...] = jnp.sin(angles)

    head_cols = H * (DN + DR)
    latent = proj[head_cols : head_cols + LAT, :].astype(jnp.bfloat16).astype(jnp.float32)
    mean_square = jnp.mean(latent * latent, axis=0, keepdims=True)
    lat_gain = jnp.broadcast_to(lat_gain_ref[...], (8, LAT)).T[:, :1]
    latent = latent * lax.rsqrt(mean_square + NORM_EPS) * lat_gain
    lat_t[...] = latent.astype(jnp.bfloat16)

    def turned(part):
        part = part.astype(jnp.bfloat16).astype(jnp.float32)
        low, high = part[: DR // 2], part[DR // 2 :]
        cosine, sine = cosine_s[...], sine_s[...]
        return jnp.concatenate(
            [low * cosine - high * sine, high * cosine + low * sine], axis=0
        )

    keys[:, :LAT] = latent.T.astype(jnp.bfloat16)
    keys[:, LAT:] = turned(proj[head_cols + LAT : head_cols + LAT + DR, :]).T.astype(jnp.bfloat16)
    q_steps[...] = jnp.zeros_like(q_steps)
    scale2 = (DN + DR) ** (-0.5) * math.log2(math.e)
    half = rows // 2
    causal = lax.broadcasted_iota(jnp.int32, (half, half), 0) <= lax.broadcasted_iota(
        jnp.int32, (half, half), 1
    )

    def attend(scores, values):
        peak = jnp.max(scores, axis=0, keepdims=True)
        weights = jnp.exp2((scores - peak) * scale2)
        weight_sum = jnp.sum(weights, axis=0, keepdims=True)
        summed = mxu(values, weights.astype(jnp.bfloat16))
        return (summed / weight_sum).astype(jnp.bfloat16)

    def uk_uv(m, hh):
        base = hh * (DN + DV)
        w_uk = jnp.concatenate(
            [ubuf[d * mp_size + m, :, base : base + DN] for d in range(dp_size)], axis=0
        )
        w_uv_t = jnp.concatenate(
            [ubuf[d * mp_size + m, :, base + DN : base + DN + DV] for d in range(dp_size)], axis=1
        )
        return w_uk, w_uv_t

    @pl.loop(4, 15)
    def _(e):
        event(1, e)

        @pl.when(e >= 11)
        def _():
            event(2, e - 11)

    @pl.loop(0, mp_size)
    def _(m):
        sibling_arrived(1, m)
        for hh in range(2):
            event(2, 4 + 2 * m + hh)
            first = pl.multiple_of(m * 2 * (DN + DR), 2 * (DN + DR)) + hh * (DN + DR)
            first = pl.multiple_of(first, 64)
            w_uk, w_uv_t = uk_uv(m, hh)
            nope = proj[pl.ds(first, DN), :].astype(jnp.bfloat16)
            q_rot = turned(proj[pl.ds(first + DN, DR), :]).astype(jnp.bfloat16)
            q_lat = mxu(w_uk, nope).astype(jnp.bfloat16)
            query = jnp.concatenate([q_lat, q_rot], axis=0)
            q_steps[...] += pltpu.roll(
                query[:, rows:].astype(jnp.float32), m * 8 + hh * 4, axis=1
            )
            scores = mxu(keys[:half, :], query[:, :half])
            low = attend(jnp.where(causal, scores, MASKED), lat_t[:, :half])
            top = mxu(keys[:half, :], query[:, half:rows])
            end = mxu(keys[half:rows, :], query[:, half:rows])
            scores = jnp.concatenate([top, jnp.where(causal, end, MASKED)], axis=0)
            high = attend(scores, lat_t[:, :rows])
            column = pl.ds(pl.multiple_of(m * 2 * DV + hh * DV, DV), DV)
            heads[:half, column] = mxu(w_uv_t, low).T.astype(jnp.bfloat16)
            heads[half:rows, column] = mxu(w_uv_t, high).T.astype(jnp.bfloat16)

    small_finish(1)
    own_keys = keys[rows : rows + STEP_ROWS, :]
    all_keys = jnp.concatenate([cbuf[m] for m in range(mp_size)] + [own_keys], axis=0)
    cached = mp_size * cache_ref.shape[0]
    column = lax.broadcasted_iota(jnp.int32, (8, cached), 1)
    request = lax.rem(lax.broadcasted_iota(jnp.int32, (8, cached), 0), requests)
    slot, entry = column // page_rows, lax.rem(column, page_rows)
    bias = jnp.full((8, cached), MASKED, jnp.float32)
    for r in range(requests):
        for page in range(table_ref.shape[1]):
            counts = (slot == table_ref[r, page]) & (page * page_rows + entry < lengths_ref[r])
            bias = jnp.where(counts & (request == r), 0.0, bias)
    own = lax.broadcasted_iota(jnp.int32, (8, STEP_ROWS), 1) == lax.rem(
        lax.broadcasted_iota(jnp.int32, (8, STEP_ROWS), 0), requests
    )
    bias = jnp.concatenate([bias, jnp.where(own, 0.0, MASKED)], axis=1)
    bias = jnp.concatenate([bias] * (STEP_LANES // 8), axis=0)
    scores = mxu(q_steps[...].T.astype(jnp.bfloat16), all_keys, NT) + bias
    peak = jnp.max(scores, axis=1, keepdims=True)
    weights = jnp.exp2((scores - peak) * scale2)
    weight_sum = jnp.sum(weights, axis=1, keepdims=True)
    summed = mxu(weights.astype(jnp.bfloat16), all_keys[:, :LAT])
    step_latent = (summed / weight_sum).astype(jnp.bfloat16)
    heads[rows:, :] = jnp.zeros((STEP_ROWS, H * DV), jnp.bfloat16)
    for h in range(H):
        _, w_uv_t = uk_uv(h // 2, h % 2)
        part = mxu(step_latent, w_uv_t, NT)
        padded = jnp.concatenate(
            [part[4 * h : 4 * h + 4], jnp.zeros((STEP_ROWS - 4, DV), jnp.float32)], axis=0
        )
        heads[rows:, h * DV : (h + 1) * DV] = padded.astype(jnp.bfloat16)

    @pl.loop(0, mp_size)
    def _(m):
        sibling_arrived(2, m)
        total = mxu(heads[:, :depth], obuf[m])
        for d in range(1, dp_size):
            total += mxu(heads[:, d * depth : (d + 1) * depth], obuf[d * mp_size + m])
        width = total.shape[1]
        done = total.astype(jnp.bfloat16)
        out_ref[:, pl.ds(pl.multiple_of(m * width, width), width)] = done[:rows]

        @pl.when(m == mp)
        def _():
            step_out_ref[...] = total[rows : rows + requests].astype(jnp.bfloat16)

    def z_sent(wait, count):
        z_neighbours(lambda i, target: wait(i))

        @pl.when(middle)
        def _():
            for e in range(z_size - 1):
                wait(count + e)

    for t in range(3):
        for hf in range(2):
            sent = lambda i: copy(t, hf, me, i, core_dev).wait_send()
            z_sent(sent, 31)

            @pl.loop(3, 31)
            def _(i):
                sent(i)

    for k in range(2):
        sent = lambda i: small(k, mp, i, y_dev).wait_send()
        z_sent(sent, 6)
        for i in range(2, 6):
            sent(i)


def fused_device(
    prompt_rows,
    step_rows,
    attn_gain,
    latent_gain,
    joined_qkva,
    kv_up,
    out_proj,
    latent_cache,
    page_table,
    cached_lengths,
):
    rows, d_model = prompt_rows.shape
    dp_size, mp_size = lax.axis_size("dp"), lax.axis_size("mp")
    block_cols = joined_qkva.shape[1]
    pad_cols = -(-block_cols // 16) * 16
    requests = step_rows.shape[0]
    slot_count, page_rows, key_width = latent_cache.shape
    lanes = rows + STEP_LANES
    sizes = (rows, dp_size, mp_size, block_cols, mp_size // 2, page_rows)
    devices = dp_size * mp_size
    bf16, f32 = jnp.bfloat16, jnp.float32
    vmem = pl.BlockSpec(memory_space=pltpu.VMEM)
    prompt_out, step_out = pl.pallas_call(
        functools.partial(fused_kernel, sizes),
        out_shape=(
            jax.ShapeDtypeStruct((rows, d_model), bf16),
            jax.ShapeDtypeStruct((requests, out_proj.shape[1]), bf16),
        ),
        in_specs=[vmem] * 8 + [pl.BlockSpec(memory_space=pltpu.SMEM)] * 2,
        out_specs=(vmem, vmem),
        scratch_shapes=[
            pltpu.VMEM((devices, pad_cols, joined_qkva.shape[0]), bf16),
            pltpu.VMEM((devices,) + kv_up.shape, bf16),
            pltpu.VMEM((devices,) + out_proj.shape, bf16),
            pltpu.VMEM((mp_size, STEP_ROWS, step_rows.shape[1]), bf16),
            pltpu.VMEM((mp_size, slot_count * page_rows, key_width), bf16),
            pltpu.VMEM((dp_size, lanes, joined_qkva.shape[0]), bf16),
            pltpu.VMEM((mp_size * block_cols, lanes), f32),
            pltpu.VMEM((LAT, lanes), bf16),
            pltpu.VMEM((lanes, LAT + DR), bf16),
            pltpu.VMEM((LAT + DR, STEP_LANES), f32),
            pltpu.VMEM((rows + STEP_ROWS, H * DV), bf16),
            pltpu.VMEM((DR // 2, lanes), f32),
            pltpu.VMEM((DR // 2, lanes), f32),
            pltpu.SemaphoreType.DMA((3, 2, 34)),
            pltpu.SemaphoreType.DMA((3, 2, devices)),
            pltpu.SemaphoreType.DMA((2, 9)),
            pltpu.SemaphoreType.DMA((2, mp_size)),
        ],
        compiler_params=pltpu.CompilerParams(
            collective_id=0, has_side_effects=True, vmem_limit_bytes=64 * 1024 * 1024
        ),
    )(
        prompt_rows,
        step_rows,
        attn_gain[None, :],
        latent_gain[None, :],
        joined_qkva.T,
        kv_up,
        out_proj,
        latent_cache.reshape(slot_count * page_rows, key_width),
        page_table,
        cached_lengths,
    )
    return prompt_out, step_out


def solution(mesh):
    placed = (
        P(("dp", "mp"), None),
        P("dp", "mp"),
        P(),
        P(),
        P("dp", "mp"),
        P("dp", "mp"),
        P("dp", "mp"),
        P(("dp", "mp"), None, None),
        P("dp", None),
        P("dp"),
    )
    fits = mesh.shape["dp"] == 4 and mesh.shape["mp"] == 8
    return jax.shard_map(
        fused_device if fits else on_device,
        mesh=mesh,
        in_specs=placed,
        out_specs=(P(("dp", "mp"), None), P("dp", "mp")),
        check_vma=False,
    )
```

```python
import functools
import math

import jax
import jax.numpy as jnp
from jax import lax
from jax.experimental import pallas as pl
from jax.experimental.pallas import tpu as pltpu
from jax.sharding import PartitionSpec as P

H = 16
DN = 128
DR = 64
DV = 128
LAT = 512
LEN = 512


NORM_EPS = 1e-06
ROPE_BASE = 50000.0
MASKED = -1e30


def merged(x, axis, combine):
    everything = jax.tree.map(
        lambda part, kind: lax.all_gather(part.astype(kind), axis),
        x,
        jax.tree.map(lambda a: jnp.bfloat16 if a.dtype == jnp.float32 else a.dtype, x),
    )

    def take(k):
        return jax.tree.map(lambda part, own: part[k].astype(own.dtype), everything, x)

    return lax.fori_loop(
        1, lax.axis_size(axis), lambda k, so_far: combine(so_far, take(k)), take(0)
    )


def rms_scale(values, scales):
    widened = values.astype(jnp.float32)
    mean_square = jnp.mean(widened * widened, axis=-1, keepdims=True)
    return widened * lax.rsqrt(mean_square + NORM_EPS) * scales


def rotate(values, positions):
    rot_width = values.shape[-1]
    half_width = rot_width // 2
    freq_steps = jnp.arange(half_width, dtype=jnp.float32)
    inv_freqs = jnp.exp(freq_steps * (-2.0 * math.log(ROPE_BASE) / rot_width))
    angles = positions.astype(jnp.float32)[:, None] * inv_freqs[None, :]
    angle_shape = (positions.shape[0],) + (1,) * (values.ndim - 2) + (half_width,)
    cosine = jnp.cos(angles).reshape(angle_shape)
    sine_part = jnp.sin(angles).reshape(angle_shape)
    lower_half = values[..., :half_width]
    upper_half = values[..., half_width:]
    return jnp.concatenate(
        [
            lower_half * cosine - upper_half * sine_part,
            upper_half * cosine + lower_half * sine_part,
        ],
        axis=-1,
    )


def queries_keys(projected, positions, latent_gain, up_heads):
    head_cols = H * (DN + DR)
    row_count = projected.shape[0]
    query_cols = projected[:, :head_cols].reshape(row_count, H, DN + DR)
    query_rot = rotate(query_cols[..., DN:].astype(jnp.float32), positions).astype(jnp.bfloat16)
    latent = rms_scale(projected[:, head_cols : head_cols + LAT], latent_gain).astype(jnp.bfloat16)
    key_rot = rotate(projected[:, head_cols + LAT :].astype(jnp.float32), positions).astype(
        jnp.bfloat16
    )
    query_lat = jnp.einsum(
        "rhn,lhn->rhl", query_cols[..., :DN], up_heads[..., :DN], preferred_element_type=jnp.float32
    ).astype(jnp.bfloat16)
    queries = jnp.concatenate([query_lat, query_rot], axis=-1)
    key_rows = jnp.concatenate([latent, key_rot], axis=-1)
    return (queries, key_rows)


def prompt_attention(queries, query_ids, all_keys, all_ids, score_scale):
    row_count = queries.shape[0]
    block_rows = min(row_count, 512)
    block_count = row_count // block_rows
    query_blocks = queries.reshape(block_count, block_rows, H, queries.shape[-1])
    id_blocks = query_ids.reshape(block_count, block_rows)
    latent_keys = all_keys[:, :LAT]

    def one_block(block_args):
        query_part, id_part = block_args
        scores = (
            jnp.einsum("qhc,kc->qhk", query_part, all_keys, preferred_element_type=jnp.float32)
            * score_scale
        )
        same_prompt = id_part[:, None] // LEN == all_ids[None, :] // LEN
        allowed = same_prompt & (all_ids[None, :] <= id_part[:, None])
        scores = jnp.where(allowed[:, None, :], scores, MASKED)
        peak_score = jnp.max(scores, axis=-1, keepdims=True)
        weights = jnp.where(allowed[:, None, :], jnp.exp(scores - peak_score), 0.0)
        weight_sum = jnp.sum(weights, axis=-1, keepdims=True)
        summed = jnp.einsum(
            "qhk,kl->qhl",
            weights.astype(jnp.bfloat16),
            latent_keys,
            preferred_element_type=jnp.float32,
        )
        return (summed / weight_sum).astype(jnp.bfloat16)

    return lax.map(one_block, (query_blocks, id_blocks)).reshape(row_count, H, LAT)


def page_attention(queries, latent_cache, page_table, cached_lengths, mp_index, score_scale):
    slot_count = latent_cache.shape[0]
    page_rows = latent_cache.shape[1]
    flat_cache = latent_cache.reshape(slot_count * page_rows, latent_cache.shape[2])
    slot_ids = mp_index * slot_count + jnp.arange(slot_count, dtype=jnp.int32)
    matches = page_table[:, :, None] == slot_ids[None, None, :]
    owned = jnp.any(matches, axis=1)
    page_numbers = jnp.arange(page_table.shape[1], dtype=jnp.int32)[None, :, None]
    page_index = jnp.sum(jnp.where(matches, page_numbers, 0), axis=1)
    key_position = (
        page_index[:, :, None] * page_rows + jnp.arange(page_rows, dtype=jnp.int32)[None, None, :]
    )
    allowed = owned[:, :, None] & (key_position < cached_lengths[:, None, None])
    allowed = allowed.reshape(page_table.shape[0], slot_count * page_rows)
    scores = (
        jnp.einsum("rhc,kc->rhk", queries, flat_cache, preferred_element_type=jnp.float32)
        * score_scale
    )
    scores = jnp.where(allowed[:, None, :], scores, MASKED)
    peak_score = jnp.max(scores, axis=-1)
    weights = jnp.where(allowed[:, None, :], jnp.exp(scores - peak_score[..., None]), 0.0)
    weight_sum = jnp.sum(weights, axis=-1)
    summed = jnp.einsum(
        "rhk,kl->rhl",
        weights.astype(jnp.bfloat16),
        flat_cache[:, :LAT],
        preferred_element_type=jnp.float32,
    )
    return (peak_score, weight_sum, summed)


def combine_partial(first_state, second_state):
    peak_score = jnp.maximum(first_state[0], second_state[0])
    first_factor = jnp.exp(first_state[0] - peak_score)
    second_factor = jnp.exp(second_state[0] - peak_score)
    weight_sum = first_state[1] * first_factor + second_state[1] * second_factor
    summed = first_state[2] * first_factor[..., None] + second_state[2] * second_factor[..., None]
    return (peak_score, weight_sum, summed)


def on_device(
    prompt_rows,
    step_rows,
    attn_gain,
    latent_gain,
    joined_qkva,
    kv_up,
    out_proj,
    latent_cache,
    page_table,
    cached_lengths,
):
    prompt_count = prompt_rows.shape[0]
    mp_index = lax.axis_index("mp")
    mp_size = lax.axis_size("mp")
    score_scale = (DN + DR) ** (-0.5)
    trainer = (
        joined_qkva.astype(jnp.bfloat16),
        kv_up.astype(jnp.bfloat16),
        out_proj.astype(jnp.bfloat16),
    )
    step_full = lax.all_gather(step_rows, "mp", axis=1, tiled=True)
    stacked = jnp.concatenate([prompt_rows, step_full], axis=0)
    normed = rms_scale(stacked, attn_gain).astype(jnp.bfloat16)
    prompt_ids = jnp.arange(prompt_count, dtype=jnp.int32)
    positions = jnp.concatenate([prompt_ids % LEN, cached_lengths], axis=0)
    served = (
        lax.all_to_all(trainer[0], "mp", split_axis=0, concat_axis=1, tiled=True),
        lax.all_to_all(trainer[1], "mp", split_axis=0, concat_axis=1, tiled=True),
        lax.all_to_all(trainer[2], "mp", split_axis=0, concat_axis=1, tiled=True),
    )
    inputs = normed
    projected = jnp.dot(
        inputs,
        lax.all_gather(served[0], ("dp", "mp"), axis=0, tiled=True),
        preferred_element_type=jnp.float32,
    )
    up_full = lax.all_gather(served[1], ("dp", "mp"), axis=0, tiled=True)
    up_heads = up_full.reshape(LAT, H, DN + DV)
    queries, key_rows = queries_keys(
        projected.astype(jnp.bfloat16), positions, latent_gain, up_heads
    )
    prompt_queries = queries[:prompt_count]
    prompt_key_rows = key_rows[:prompt_count]
    step_queries = queries[prompt_count:]
    step_keys = key_rows[prompt_count:]
    prompt_latent = prompt_attention(
        prompt_queries, prompt_ids, prompt_key_rows, prompt_ids, score_scale
    )
    partial_state = page_attention(
        step_queries, latent_cache, page_table, cached_lengths, mp_index, score_scale
    )
    peak_score, weight_sum, summed = merged(partial_state, "mp", combine_partial)
    own_score = (
        jnp.einsum("rhc,rc->rh", step_queries, step_keys, preferred_element_type=jnp.float32)
        * score_scale
    )
    new_peak = jnp.maximum(peak_score, own_score)
    old_factor = jnp.exp(peak_score - new_peak)
    own_weight = jnp.exp(own_score - new_peak)
    weight_sum = weight_sum * old_factor + own_weight
    own_latent = step_keys[:, :LAT].astype(jnp.float32)
    own_half = own_weight.astype(jnp.bfloat16).astype(jnp.float32)
    summed = summed * old_factor[..., None] + own_half[..., None] * own_latent[:, None, :]
    step_latent = (summed / weight_sum[..., None]).astype(jnp.bfloat16)
    latent_out = jnp.concatenate([prompt_latent, step_latent], axis=0)
    heads_out = jnp.einsum(
        "rhl,lhv->rhv", latent_out, up_heads[..., DN:], preferred_element_type=jnp.float32
    ).astype(jnp.bfloat16)
    heads_out = heads_out.reshape(latent_out.shape[0], H * DV)
    inputs = heads_out
    attended = jnp.dot(
        inputs,
        lax.all_gather(served[2], ("dp", "mp"), axis=0, tiled=True),
        preferred_element_type=jnp.float32,
    )
    attended = attended.astype(jnp.bfloat16)
    prompt_out = attended[:prompt_count]
    col_width = attended.shape[1] // mp_size
    step_out = lax.dynamic_slice_in_dim(attended[prompt_count:], mp_index * col_width, col_width, 1)
    return (prompt_out, step_out)


MESH = pl.DeviceIdType.MESH
STEP_LANES = 128
STEP_ROWS = 16
NN = (((1,), (0,)), ((), ()))
NT = (((1,), (1,)), ((), ()))


def mxu(a, b, dims=NN):
    return lax.dot_general(a, b, dims, preferred_element_type=jnp.float32)


def fused_kernel(
    sizes,
    x_ref,
    step_ref,
    gain_ref,
    lat_gain_ref,
    joined_ref,
    up_ref,
    out_w_ref,
    cache_ref,
    table_ref,
    lengths_ref,
    out_ref,
    step_out_ref,
    jbuf,
    ubuf,
    obuf,
    sbuf,
    cbuf,
    normed,
    proj,
    lat_t,
    keys,
    q_steps,
    heads,
    cosine_s,
    sine_s,
    send_sem,
    recv_sem,
    small_send,
    small_recv,
):
    rows, dp_size, mp_size, block_cols, z_size, page_rows = sizes
    dp = lax.axis_index("dp")
    mp = lax.axis_index("mp")
    x, core = dp // 2, dp % 2
    z, y = mp // 2, mp % 2
    bufs = (jbuf, ubuf, obuf)
    pad_cols = jbuf.shape[1]
    cuts = tuple(
        (0, (buf.shape[1] * 59 // 1600) * 16, buf.shape[1]) for buf in bufs
    )
    depth = normed.shape[2]
    requests = step_ref.shape[0]
    lanes = rows + STEP_LANES

    def dev(xx, cc, yy, zz):
        return (xx * 2 + cc, zz * 2 + yy)

    def slot_of(xx, cc, yy, zz):
        return (xx * 2 + cc) * mp_size + zz * 2 + yy

    me = slot_of(x, core, y, z)
    y_dev = dev(x, core, 1 - y, z)
    x_dev = dev(1 - x, core, y, z)
    core_dev = dev(x, 1 - core, y, z)

    middle = (z == 1) | (z == 2)

    def z_at(n):
        far = z // 2
        inner = lax.rem(lax.rem(z + 1, z_size) // 2, 2)
        place = (1 - inner) * n + inner * (lax.rem(n + 1, 3) + n // 3 * 2)
        return (1 - far) * place + far * (z_size - 1 - place)

    def z_next(e):
        odd = lax.rem(e, 2)
        return dev(x, core, y, (1 - odd) * 3 * (z - 1) + odd * (3 - z))

    def z_neighbours(act):
        @pl.when(z > 0)
        def _():
            act(0, dev(x, core, y, z - 1))

        @pl.when(z < z_size - 1)
        def _():
            act(1, dev(x, core, y, z + 1))

    barrier = pltpu.get_barrier_semaphore()

    def greet(_, friend):
        pl.semaphore_signal(barrier, inc=1, device_id=friend, device_id_type=MESH)

    z_neighbours(greet)
    for friend in (y_dev, x_dev, core_dev):
        greet(None, friend)

    def copy(t, hf, slot, index, target):
        lo, hi = cuts[t][hf], cuts[t][hf + 1]
        ref = bufs[t].at[slot, pl.ds(lo, hi - lo)]
        return pltpu.make_async_remote_copy(
            src_ref=ref,
            dst_ref=ref,
            send_sem=send_sem.at[t, hf, index],
            recv_sem=recv_sem.at[t, hf, slot],
            device_id=target,
            device_id_type=MESH,
        )

    def arrived(t, hf, slot):
        copy(t, hf, slot, 0, core_dev).wait_recv()

    axis_devs = ((y_dev, x_dev), (x_dev, y_dev))

    def begin(t):
        for hf in range(2):
            z_neighbours(lambda i, target: copy(t, hf, me, i, target).start())
            copy(t, hf, me, 3, axis_devs[hf][0]).start()
            copy(t, hf, me, 7, axis_devs[hf][1]).start()
            copy(t, hf, me, 15, core_dev).start()

    def near(hf, zz, first, second):
        if hf == 0:
            return slot_of(second, core, first, zz)
        return slot_of(first, core, second, zz)

    def event(t, e):
        @pl.when(e < 3)
        def _():
            for hf in range(2):
                slot = slot_of(x, core, y, z_at(e + 1))
                arrived(t, hf, slot)

                @pl.when(middle)
                def _():
                    copy(t, hf, slot, 31 + e, z_next(e)).start()

                copy(t, hf, slot, 4 + e, axis_devs[hf][0]).start()
                copy(t, hf, slot, 8 + e, axis_devs[hf][1]).start()
                copy(t, hf, slot, 16 + e, core_dev).start()

        @pl.when((e >= 3) & (e < 7))
        def _():
            j = e - 3
            zz = z_at(j)
            for hf in range(2):
                slot = near(hf, zz, 1 - (y, x)[hf], (x, y)[hf])
                arrived(t, hf, slot)
                copy(t, hf, slot, 11 + j, axis_devs[hf][1]).start()
                copy(t, hf, slot, 19 + j, core_dev).start()

        @pl.when((e >= 7) & (e < 15))
        def _():
            j = e - 7
            zz = z_at(lax.rem(j, z_size))
            for hf in range(2):
                first = lax.rem((y, x)[hf] + j // z_size, 2)
                slot = near(hf, zz, first, 1 - (x, y)[hf])
                arrived(t, hf, slot)
                copy(t, hf, slot, 23 + j, core_dev).start()

    def small(k, slot, index, target):
        ref = (sbuf, cbuf)[k].at[slot]
        return pltpu.make_async_remote_copy(
            src_ref=ref,
            dst_ref=ref,
            send_sem=small_send.at[k, index],
            recv_sem=small_recv.at[k, slot],
            device_id=target,
            device_id_type=MESH,
        )

    def small_begin(k):
        z_neighbours(lambda i, target: small(k, mp, i, target).start())
        small(k, mp, 2, y_dev).start()

    def small_forward(k):
        for e in range(z_size - 1):
            slot = z_at(e + 1) * 2 + y
            small(k, slot, 0, y_dev).wait_recv()

            @pl.when(middle)
            def _():
                small(k, slot, 6 + e, z_next(e)).start()

            small(k, slot, 3 + e, y_dev).start()

    def small_finish(k):
        for j in range(z_size):
            slot = z_at(j) * 2 + 1 - y
            small(k, slot, 0, y_dev).wait_recv()

    jbuf[me] = jnp.concatenate(
        [joined_ref[...], jnp.zeros((pad_cols - block_cols, depth), jnp.float32)], axis=0
    ).astype(jnp.bfloat16)
    sbuf[mp] = jnp.concatenate(
        [
            step_ref[...].astype(jnp.float32),
            jnp.zeros((STEP_ROWS - requests, step_ref.shape[1]), jnp.float32),
        ],
        axis=0,
    ).astype(jnp.bfloat16)
    pl.semaphore_wait(barrier, 4 + lax.rem((z + 1) // 2, 2))
    small_begin(0)
    begin(0)

    for hh in range(2):
        base = hh * (DN + DV)
        ubuf[me, :, base : base + DN] = up_ref[:, base : base + DN].astype(jnp.bfloat16)
        ubuf[me, :, base + DN : base + DN + DV] = (
            up_ref[:, base + DN : base + DN + DV].T.astype(jnp.bfloat16)
        )
    obuf[me] = out_w_ref[...].astype(jnp.bfloat16)
    cbuf[mp] = cache_ref[...]
    small_forward(0)

    @pl.loop(0, rows // 64)
    def _(i):
        at = pl.ds(pl.multiple_of(i * 64, 64), 64)
        part = rms_scale(x_ref[at, :], gain_ref[...]).astype(jnp.bfloat16)
        for d in range(dp_size):
            normed[d, at, :] = part[:, d * depth : (d + 1) * depth]

    @pl.loop(0, proj.shape[0] // 64)
    def _(i):
        proj[pl.ds(pl.multiple_of(i * 64, 64), 64), :] = jnp.zeros((64, lanes), jnp.float32)

    small_finish(0)
    step_full = jnp.concatenate([sbuf[m] for m in range(mp_size)], axis=1)
    part = rms_scale(step_full, gain_ref[...]).astype(jnp.bfloat16)
    for d in range(dp_size):
        normed[d, rows : rows + STEP_ROWS, :] = part[:, d * depth : (d + 1) * depth]
        normed[d, rows + STEP_ROWS :, :] = jnp.zeros((STEP_LANES - STEP_ROWS, depth), jnp.bfloat16)

    def slot_at(hf, n, cc):
        zz = z_at(n % 4)
        first = lax.rem((y, x)[hf] + n // 4, 2)
        second = lax.rem((x, y)[hf] + n // 8, 2)
        if hf == 0:
            return slot_of(second, cc, first, zz)
        return slot_of(first, cc, second, zz)

    def project(n, cc, wait):
        for hf in range(2):
            slot = slot_at(hf, n, cc)
            if wait:
                arrived(0, hf, slot)
            lo, hi = cuts[0][hf], cuts[0][hf + 1]
            valid = min(hi, block_cols) - lo
            total = mxu(jbuf[slot, lo:hi, :], normed[slot // mp_size], NT)
            at = pl.ds(pl.multiple_of(lax.rem(slot, mp_size) * block_cols + lo, 8), valid)
            proj[at, :] += total[:valid]

    project(0, core, False)

    @pl.loop(1, 16)
    def _(n):
        event(0, n - 1)

        @pl.when(n == 7)
        def _():
            begin(1)
            small_begin(1)

        @pl.when(n >= 12)
        def _():
            event(1, n - 12)

        project(n, core, False)
        project(n - 1, 1 - core, True)

    begin(2)

    @pl.loop(4, 7)
    def _(e):
        event(1, e)

    small_forward(1)
    project(15, 1 - core, True)

    def sibling_arrived(t, m):
        for xx in range(2):
            for hf in range(2):
                arrived(t, hf, (xx * 2 + 1 - core) * mp_size + m)

    lane = lax.broadcasted_iota(jnp.int32, (DR // 2, lanes), 1)
    positions = jnp.where(lane < rows, lane, 0)
    for r in range(requests):
        positions = jnp.where(lane == rows + r, lengths_ref[r], positions)
    step = lax.broadcasted_iota(jnp.int32, (DR // 2, lanes), 0).astype(jnp.float32)
    angles = positions.astype(jnp.float32) * jnp.exp(step * (-2.0 * math.log(ROPE_BASE) / DR))
    cosine_s[...] = jnp.cos(angles)
    sine_s[...] = jnp.sin(angles)

    head_cols = H * (DN + DR)
    latent = proj[head_cols : head_cols + LAT, :].astype(jnp.bfloat16).astype(jnp.float32)
    mean_square = jnp.mean(latent * latent, axis=0, keepdims=True)
    lat_gain = jnp.broadcast_to(lat_gain_ref[...], (8, LAT)).T[:, :1]
    latent = latent * lax.rsqrt(mean_square + NORM_EPS) * lat_gain
    lat_t[...] = latent.astype(jnp.bfloat16)

    def turned(part):
        part = part.astype(jnp.bfloat16).astype(jnp.float32)
        low, high = part[: DR // 2], part[DR // 2 :]
        cosine, sine = cosine_s[...], sine_s[...]
        return jnp.concatenate(
            [low * cosine - high * sine, high * cosine + low * sine], axis=0
        )

    keys[:, :LAT] = latent.T.astype(jnp.bfloat16)
    keys[:, LAT:] = turned(proj[head_cols + LAT : head_cols + LAT + DR, :]).T.astype(jnp.bfloat16)
    q_steps[...] = jnp.zeros_like(q_steps)
    scale2 = (DN + DR) ** (-0.5) * math.log2(math.e)
    half = rows // 2
    causal = lax.broadcasted_iota(jnp.int32, (half, half), 0) <= lax.broadcasted_iota(
        jnp.int32, (half, half), 1
    )

    def attend(scores, values):
        peak = jnp.max(scores, axis=0, keepdims=True)
        weights = jnp.exp2((scores - peak) * scale2)
        weight_sum = jnp.sum(weights, axis=0, keepdims=True)
        summed = mxu(values, weights.astype(jnp.bfloat16))
        return (summed * (1.0 / weight_sum)).astype(jnp.bfloat16)

    def uk_uv(m, hh):
        base = hh * (DN + DV)
        w_uk = jnp.concatenate(
            [ubuf[d * mp_size + m, :, base : base + DN] for d in range(dp_size)], axis=0
        )
        w_uv_t = jnp.concatenate(
            [ubuf[d * mp_size + m, :, base + DN : base + DN + DV] for d in range(dp_size)], axis=1
        )
        return w_uk, w_uv_t

    @pl.loop(0, mp_size)
    def _(k):
        event(1, 7 + k)
        m = z_at(lax.rem(k, z_size)) * 2 + lax.rem(y + k // z_size, 2)
        sibling_arrived(1, m)
        for hh in range(2):
            event(2, 2 * k + hh)
            first = pl.multiple_of(m * 2 * (DN + DR), 2 * (DN + DR)) + hh * (DN + DR)
            first = pl.multiple_of(first, 64)
            w_uk, w_uv_t = uk_uv(m, hh)
            nope = proj[pl.ds(first, DN), :].astype(jnp.bfloat16)
            q_rot = turned(proj[pl.ds(first + DN, DR), :]).astype(jnp.bfloat16)
            q_lat = mxu(w_uk, nope).astype(jnp.bfloat16)
            query = jnp.concatenate([q_lat, q_rot], axis=0)
            q_steps[...] += pltpu.roll(
                query[:, rows:].astype(jnp.float32), m * 8 + hh * 4, axis=1
            )
            scores = mxu(keys[:half, :], query[:, :half])
            low = attend(jnp.where(causal, scores, MASKED), lat_t[:, :half])
            top = mxu(keys[:half, :], query[:, half:rows])
            end = mxu(keys[half:rows, :], query[:, half:rows])
            scores = jnp.concatenate([top, jnp.where(causal, end, MASKED)], axis=0)
            high = attend(scores, lat_t[:, :rows])
            column = pl.ds(pl.multiple_of(m * 2 * DV + hh * DV, DV), DV)
            heads[:half, column] = mxu(w_uv_t, low).T.astype(jnp.bfloat16)
            heads[half:rows, column] = mxu(w_uv_t, high).T.astype(jnp.bfloat16)

    small_finish(1)
    own_keys = keys[rows : rows + STEP_ROWS, :]
    all_keys = jnp.concatenate([cbuf[m] for m in range(mp_size)] + [own_keys], axis=0)
    cached = mp_size * cache_ref.shape[0]
    column = lax.broadcasted_iota(jnp.int32, (8, cached), 1)
    request = lax.rem(lax.broadcasted_iota(jnp.int32, (8, cached), 0), requests)
    slot, entry = column // page_rows, lax.rem(column, page_rows)
    bias = jnp.full((8, cached), MASKED, jnp.float32)
    for r in range(requests):
        for page in range(table_ref.shape[1]):
            counts = (slot == table_ref[r, page]) & (page * page_rows + entry < lengths_ref[r])
            bias = jnp.where(counts & (request == r), 0.0, bias)
    own = lax.broadcasted_iota(jnp.int32, (8, STEP_ROWS), 1) == lax.rem(
        lax.broadcasted_iota(jnp.int32, (8, STEP_ROWS), 0), requests
    )
    bias = jnp.concatenate([bias, jnp.where(own, 0.0, MASKED)], axis=1)
    live = H * requests
    bias = jnp.concatenate([bias] * (live // 8), axis=0)
    scores = mxu(q_steps[...].T[:live].astype(jnp.bfloat16), all_keys, NT) + bias
    peak = jnp.max(scores, axis=1, keepdims=True)
    weights = jnp.exp2((scores - peak) * scale2)
    weight_sum = jnp.sum(weights, axis=1, keepdims=True)
    summed = mxu(weights.astype(jnp.bfloat16), all_keys[:, :LAT])
    step_latent = (summed / weight_sum).astype(jnp.bfloat16)
    heads[rows:, :] = jnp.zeros((STEP_ROWS, H * DV), jnp.bfloat16)
    for h in range(H):
        _, w_uv_t = uk_uv(h // 2, h % 2)
        part = mxu(step_latent, w_uv_t, NT)
        padded = jnp.concatenate(
            [part[4 * h : 4 * h + 4], jnp.zeros((STEP_ROWS - 4, DV), jnp.float32)], axis=0
        )
        heads[rows:, h * DV : (h + 1) * DV] = padded.astype(jnp.bfloat16)

    @pl.loop(0, mp_size)
    def _(m):
        sibling_arrived(2, m)
        total = mxu(heads[:, :depth], obuf[m])
        for d in range(1, dp_size):
            total += mxu(heads[:, d * depth : (d + 1) * depth], obuf[d * mp_size + m])
        width = total.shape[1]
        done = total.astype(jnp.bfloat16)
        out_ref[:, pl.ds(pl.multiple_of(m * width, width), width)] = done[:rows]

        @pl.when(m == mp)
        def _():
            step_out_ref[...] = total[rows : rows + requests].astype(jnp.bfloat16)

    def z_sent(wait, count):
        z_neighbours(lambda i, target: wait(i))

        @pl.when(middle)
        def _():
            for e in range(z_size - 1):
                wait(count + e)

    for t in range(3):
        for hf in range(2):
            sent = lambda i: copy(t, hf, me, i, core_dev).wait_send()
            z_sent(sent, 31)

            @pl.loop(3, 31)
            def _(i):
                sent(i)

    for k in range(2):
        sent = lambda i: small(k, mp, i, y_dev).wait_send()
        z_sent(sent, 6)
        for i in range(2, 6):
            sent(i)


def fused_device(
    prompt_rows,
    step_rows,
    attn_gain,
    latent_gain,
    joined_qkva,
    kv_up,
    out_proj,
    latent_cache,
    page_table,
    cached_lengths,
):
    rows, d_model = prompt_rows.shape
    dp_size, mp_size = lax.axis_size("dp"), lax.axis_size("mp")
    block_cols = joined_qkva.shape[1]
    pad_cols = -(-block_cols // 16) * 16
    requests = step_rows.shape[0]
    slot_count, page_rows, key_width = latent_cache.shape
    lanes = rows + STEP_LANES
    sizes = (rows, dp_size, mp_size, block_cols, mp_size // 2, page_rows)
    devices = dp_size * mp_size
    bf16, f32 = jnp.bfloat16, jnp.float32
    vmem = pl.BlockSpec(memory_space=pltpu.VMEM)
    prompt_out, step_out = pl.pallas_call(
        functools.partial(fused_kernel, sizes),
        out_shape=(
            jax.ShapeDtypeStruct((rows, d_model), bf16),
            jax.ShapeDtypeStruct((requests, out_proj.shape[1]), bf16),
        ),
        in_specs=[vmem] * 8 + [pl.BlockSpec(memory_space=pltpu.SMEM)] * 2,
        out_specs=(vmem, vmem),
        scratch_shapes=[
            pltpu.VMEM((devices, pad_cols, joined_qkva.shape[0]), bf16),
            pltpu.VMEM((devices,) + kv_up.shape, bf16),
            pltpu.VMEM((devices,) + out_proj.shape, bf16),
            pltpu.VMEM((mp_size, STEP_ROWS, step_rows.shape[1]), bf16),
            pltpu.VMEM((mp_size, slot_count * page_rows, key_width), bf16),
            pltpu.VMEM((dp_size, lanes, joined_qkva.shape[0]), bf16),
            pltpu.VMEM((mp_size * block_cols, lanes), f32),
            pltpu.VMEM((LAT, lanes), bf16),
            pltpu.VMEM((lanes, LAT + DR), bf16),
            pltpu.VMEM((LAT + DR, STEP_LANES), f32),
            pltpu.VMEM((rows + STEP_ROWS, H * DV), bf16),
            pltpu.VMEM((DR // 2, lanes), f32),
            pltpu.VMEM((DR // 2, lanes), f32),
            pltpu.SemaphoreType.DMA((3, 2, 34)),
            pltpu.SemaphoreType.DMA((3, 2, devices)),
            pltpu.SemaphoreType.DMA((2, 9)),
            pltpu.SemaphoreType.DMA((2, mp_size)),
        ],
        compiler_params=pltpu.CompilerParams(
            collective_id=0, has_side_effects=True, vmem_limit_bytes=64 * 1024 * 1024
        ),
    )(
        prompt_rows,
        step_rows,
        attn_gain[None, :],
        latent_gain[None, :],
        joined_qkva.T,
        kv_up,
        out_proj,
        latent_cache.reshape(slot_count * page_rows, key_width),
        page_table,
        cached_lengths,
    )
    return prompt_out, step_out


def solution(mesh):
    placed = (
        P(("dp", "mp"), None),
        P("dp", "mp"),
        P(),
        P(),
        P("dp", "mp"),
        P("dp", "mp"),
        P("dp", "mp"),
        P(("dp", "mp"), None, None),
        P("dp", None),
        P("dp"),
    )
    fits = mesh.shape["dp"] == 4 and mesh.shape["mp"] == 8
    return jax.shard_map(
        fused_device if fits else on_device,
        mesh=mesh,
        in_specs=placed,
        out_specs=(P(("dp", "mp"), None), P("dp", "mp")),
        check_vma=False,
    )
```

```python
import functools
import math

import jax
import jax.numpy as jnp
from jax import lax
from jax.experimental import pallas as pl
from jax.experimental.pallas import tpu as pltpu
from jax.sharding import PartitionSpec as P

H = 16
DN = 128
DR = 64
DV = 128
LAT = 512
LEN = 512


NORM_EPS = 1e-06
ROPE_BASE = 50000.0
MASKED = -1e30


def merged(x, axis, combine):
    everything = jax.tree.map(
        lambda part, kind: lax.all_gather(part.astype(kind), axis),
        x,
        jax.tree.map(lambda a: jnp.bfloat16 if a.dtype == jnp.float32 else a.dtype, x),
    )

    def take(k):
        return jax.tree.map(lambda part, own: part[k].astype(own.dtype), everything, x)

    return lax.fori_loop(
        1, lax.axis_size(axis), lambda k, so_far: combine(so_far, take(k)), take(0)
    )


def rms_scale(values, scales):
    widened = values.astype(jnp.float32)
    mean_square = jnp.mean(widened * widened, axis=-1, keepdims=True)
    return widened * lax.rsqrt(mean_square + NORM_EPS) * scales


def rotate(values, positions):
    rot_width = values.shape[-1]
    half_width = rot_width // 2
    freq_steps = jnp.arange(half_width, dtype=jnp.float32)
    inv_freqs = jnp.exp(freq_steps * (-2.0 * math.log(ROPE_BASE) / rot_width))
    angles = positions.astype(jnp.float32)[:, None] * inv_freqs[None, :]
    angle_shape = (positions.shape[0],) + (1,) * (values.ndim - 2) + (half_width,)
    cosine = jnp.cos(angles).reshape(angle_shape)
    sine_part = jnp.sin(angles).reshape(angle_shape)
    lower_half = values[..., :half_width]
    upper_half = values[..., half_width:]
    return jnp.concatenate(
        [
            lower_half * cosine - upper_half * sine_part,
            upper_half * cosine + lower_half * sine_part,
        ],
        axis=-1,
    )


def queries_keys(projected, positions, latent_gain, up_heads):
    head_cols = H * (DN + DR)
    row_count = projected.shape[0]
    query_cols = projected[:, :head_cols].reshape(row_count, H, DN + DR)
    query_rot = rotate(query_cols[..., DN:].astype(jnp.float32), positions).astype(jnp.bfloat16)
    latent = rms_scale(projected[:, head_cols : head_cols + LAT], latent_gain).astype(jnp.bfloat16)
    key_rot = rotate(projected[:, head_cols + LAT :].astype(jnp.float32), positions).astype(
        jnp.bfloat16
    )
    query_lat = jnp.einsum(
        "rhn,lhn->rhl", query_cols[..., :DN], up_heads[..., :DN], preferred_element_type=jnp.float32
    ).astype(jnp.bfloat16)
    queries = jnp.concatenate([query_lat, query_rot], axis=-1)
    key_rows = jnp.concatenate([latent, key_rot], axis=-1)
    return (queries, key_rows)


def prompt_attention(queries, query_ids, all_keys, all_ids, score_scale):
    row_count = queries.shape[0]
    block_rows = min(row_count, 512)
    block_count = row_count // block_rows
    query_blocks = queries.reshape(block_count, block_rows, H, queries.shape[-1])
    id_blocks = query_ids.reshape(block_count, block_rows)
    latent_keys = all_keys[:, :LAT]

    def one_block(block_args):
        query_part, id_part = block_args
        scores = (
            jnp.einsum("qhc,kc->qhk", query_part, all_keys, preferred_element_type=jnp.float32)
            * score_scale
        )
        same_prompt = id_part[:, None] // LEN == all_ids[None, :] // LEN
        allowed = same_prompt & (all_ids[None, :] <= id_part[:, None])
        scores = jnp.where(allowed[:, None, :], scores, MASKED)
        peak_score = jnp.max(scores, axis=-1, keepdims=True)
        weights = jnp.where(allowed[:, None, :], jnp.exp(scores - peak_score), 0.0)
        weight_sum = jnp.sum(weights, axis=-1, keepdims=True)
        summed = jnp.einsum(
            "qhk,kl->qhl",
            weights.astype(jnp.bfloat16),
            latent_keys,
            preferred_element_type=jnp.float32,
        )
        return (summed / weight_sum).astype(jnp.bfloat16)

    return lax.map(one_block, (query_blocks, id_blocks)).reshape(row_count, H, LAT)


def page_attention(queries, latent_cache, page_table, cached_lengths, mp_index, score_scale):
    slot_count = latent_cache.shape[0]
    page_rows = latent_cache.shape[1]
    flat_cache = latent_cache.reshape(slot_count * page_rows, latent_cache.shape[2])
    slot_ids = mp_index * slot_count + jnp.arange(slot_count, dtype=jnp.int32)
    matches = page_table[:, :, None] == slot_ids[None, None, :]
    owned = jnp.any(matches, axis=1)
    page_numbers = jnp.arange(page_table.shape[1], dtype=jnp.int32)[None, :, None]
    page_index = jnp.sum(jnp.where(matches, page_numbers, 0), axis=1)
    key_position = (
        page_index[:, :, None] * page_rows + jnp.arange(page_rows, dtype=jnp.int32)[None, None, :]
    )
    allowed = owned[:, :, None] & (key_position < cached_lengths[:, None, None])
    allowed = allowed.reshape(page_table.shape[0], slot_count * page_rows)
    scores = (
        jnp.einsum("rhc,kc->rhk", queries, flat_cache, preferred_element_type=jnp.float32)
        * score_scale
    )
    scores = jnp.where(allowed[:, None, :], scores, MASKED)
    peak_score = jnp.max(scores, axis=-1)
    weights = jnp.where(allowed[:, None, :], jnp.exp(scores - peak_score[..., None]), 0.0)
    weight_sum = jnp.sum(weights, axis=-1)
    summed = jnp.einsum(
        "rhk,kl->rhl",
        weights.astype(jnp.bfloat16),
        flat_cache[:, :LAT],
        preferred_element_type=jnp.float32,
    )
    return (peak_score, weight_sum, summed)


def combine_partial(first_state, second_state):
    peak_score = jnp.maximum(first_state[0], second_state[0])
    first_factor = jnp.exp(first_state[0] - peak_score)
    second_factor = jnp.exp(second_state[0] - peak_score)
    weight_sum = first_state[1] * first_factor + second_state[1] * second_factor
    summed = first_state[2] * first_factor[..., None] + second_state[2] * second_factor[..., None]
    return (peak_score, weight_sum, summed)


def on_device(
    prompt_rows,
    step_rows,
    attn_gain,
    latent_gain,
    joined_qkva,
    kv_up,
    out_proj,
    latent_cache,
    page_table,
    cached_lengths,
):
    prompt_count = prompt_rows.shape[0]
    mp_index = lax.axis_index("mp")
    mp_size = lax.axis_size("mp")
    score_scale = (DN + DR) ** (-0.5)
    trainer = (
        joined_qkva.astype(jnp.bfloat16),
        kv_up.astype(jnp.bfloat16),
        out_proj.astype(jnp.bfloat16),
    )
    step_full = lax.all_gather(step_rows, "mp", axis=1, tiled=True)
    stacked = jnp.concatenate([prompt_rows, step_full], axis=0)
    normed = rms_scale(stacked, attn_gain).astype(jnp.bfloat16)
    prompt_ids = jnp.arange(prompt_count, dtype=jnp.int32)
    positions = jnp.concatenate([prompt_ids % LEN, cached_lengths], axis=0)
    served = (
        lax.all_to_all(trainer[0], "mp", split_axis=0, concat_axis=1, tiled=True),
        lax.all_to_all(trainer[1], "mp", split_axis=0, concat_axis=1, tiled=True),
        lax.all_to_all(trainer[2], "mp", split_axis=0, concat_axis=1, tiled=True),
    )
    inputs = normed
    projected = jnp.dot(
        inputs,
        lax.all_gather(served[0], ("dp", "mp"), axis=0, tiled=True),
        preferred_element_type=jnp.float32,
    )
    up_full = lax.all_gather(served[1], ("dp", "mp"), axis=0, tiled=True)
    up_heads = up_full.reshape(LAT, H, DN + DV)
    queries, key_rows = queries_keys(
        projected.astype(jnp.bfloat16), positions, latent_gain, up_heads
    )
    prompt_queries = queries[:prompt_count]
    prompt_key_rows = key_rows[:prompt_count]
    step_queries = queries[prompt_count:]
    step_keys = key_rows[prompt_count:]
    prompt_latent = prompt_attention(
        prompt_queries, prompt_ids, prompt_key_rows, prompt_ids, score_scale
    )
    partial_state = page_attention(
        step_queries, latent_cache, page_table, cached_lengths, mp_index, score_scale
    )
    peak_score, weight_sum, summed = merged(partial_state, "mp", combine_partial)
    own_score = (
        jnp.einsum("rhc,rc->rh", step_queries, step_keys, preferred_element_type=jnp.float32)
        * score_scale
    )
    new_peak = jnp.maximum(peak_score, own_score)
    old_factor = jnp.exp(peak_score - new_peak)
    own_weight = jnp.exp(own_score - new_peak)
    weight_sum = weight_sum * old_factor + own_weight
    own_latent = step_keys[:, :LAT].astype(jnp.float32)
    own_half = own_weight.astype(jnp.bfloat16).astype(jnp.float32)
    summed = summed * old_factor[..., None] + own_half[..., None] * own_latent[:, None, :]
    step_latent = (summed / weight_sum[..., None]).astype(jnp.bfloat16)
    latent_out = jnp.concatenate([prompt_latent, step_latent], axis=0)
    heads_out = jnp.einsum(
        "rhl,lhv->rhv", latent_out, up_heads[..., DN:], preferred_element_type=jnp.float32
    ).astype(jnp.bfloat16)
    heads_out = heads_out.reshape(latent_out.shape[0], H * DV)
    inputs = heads_out
    attended = jnp.dot(
        inputs,
        lax.all_gather(served[2], ("dp", "mp"), axis=0, tiled=True),
        preferred_element_type=jnp.float32,
    )
    attended = attended.astype(jnp.bfloat16)
    prompt_out = attended[:prompt_count]
    col_width = attended.shape[1] // mp_size
    step_out = lax.dynamic_slice_in_dim(attended[prompt_count:], mp_index * col_width, col_width, 1)
    return (prompt_out, step_out)


MESH = pl.DeviceIdType.MESH
STEP_LANES = 128
STEP_ROWS = 16
NN = (((1,), (0,)), ((), ()))
NT = (((1,), (1,)), ((), ()))


def mxu(a, b, dims=NN):
    return lax.dot_general(a, b, dims, preferred_element_type=jnp.float32)


def fused_kernel(
    sizes,
    x_ref,
    step_ref,
    gain_ref,
    lat_gain_ref,
    joined_ref,
    up_ref,
    out_w_ref,
    cache_ref,
    table_ref,
    lengths_ref,
    out_ref,
    step_out_ref,
    jbuf,
    ubuf,
    obuf,
    sbuf,
    cbuf,
    normed,
    proj,
    lat_t,
    keys,
    q_steps,
    heads,
    cosine_s,
    sine_s,
    send_sem,
    recv_sem,
    small_send,
    small_recv,
):
    rows, dp_size, mp_size, block_cols, z_size, page_rows = sizes
    dp = lax.axis_index("dp")
    mp = lax.axis_index("mp")
    x, core = dp // 2, dp % 2
    z, y = mp // 2, mp % 2
    bufs = (jbuf, ubuf, obuf)
    pad_cols = jbuf.shape[1]
    cuts = tuple(
        (0, (buf.shape[1] * 59 // 1600) * 16, buf.shape[1]) for buf in bufs
    )
    depth = normed.shape[2]
    requests = step_ref.shape[0]
    lanes = rows + STEP_LANES

    def dev(xx, cc, yy, zz):
        return (xx * 2 + cc, zz * 2 + yy)

    def slot_of(xx, cc, yy, zz):
        return (xx * 2 + cc) * mp_size + zz * 2 + yy

    me = slot_of(x, core, y, z)
    y_dev = dev(x, core, 1 - y, z)
    x_dev = dev(1 - x, core, y, z)
    core_dev = dev(x, 1 - core, y, z)

    middle = (z == 1) | (z == 2)

    def z_at(n):
        far = z // 2
        inner = lax.rem(lax.rem(z + 1, z_size) // 2, 2)
        place = (1 - inner) * n + inner * (lax.rem(n + 1, 3) + n // 3 * 2)
        return (1 - far) * place + far * (z_size - 1 - place)

    def z_next(e):
        odd = lax.rem(e, 2)
        return dev(x, core, y, (1 - odd) * 3 * (z - 1) + odd * (3 - z))

    def z_neighbours(act):
        @pl.when(z > 0)
        def _():
            act(0, dev(x, core, y, z - 1))

        @pl.when(z < z_size - 1)
        def _():
            act(1, dev(x, core, y, z + 1))

    barrier = pltpu.get_barrier_semaphore()

    def greet(_, friend):
        pl.semaphore_signal(barrier, inc=1, device_id=friend, device_id_type=MESH)

    z_neighbours(greet)
    for friend in (y_dev, x_dev, core_dev):
        greet(None, friend)

    def copy(t, hf, slot, index, target):
        lo, hi = cuts[t][hf], cuts[t][hf + 1]
        ref = bufs[t].at[slot, pl.ds(lo, hi - lo)]
        return pltpu.make_async_remote_copy(
            src_ref=ref,
            dst_ref=ref,
            send_sem=send_sem.at[t, hf, index],
            recv_sem=recv_sem.at[t, hf, slot],
            device_id=target,
            device_id_type=MESH,
        )

    def arrived(t, hf, slot):
        copy(t, hf, slot, 0, core_dev).wait_recv()

    axis_devs = ((y_dev, x_dev), (x_dev, y_dev))

    def begin(t):
        for hf in range(2):
            z_neighbours(lambda i, target: copy(t, hf, me, i, target).start())
            copy(t, hf, me, 3, axis_devs[hf][0]).start()
            copy(t, hf, me, 7, axis_devs[hf][1]).start()
            copy(t, hf, me, 15, core_dev).start()

    def near(hf, zz, first, second):
        if hf == 0:
            return slot_of(second, core, first, zz)
        return slot_of(first, core, second, zz)

    def event(t, e):
        @pl.when(e < 3)
        def _():
            for hf in range(2):
                slot = slot_of(x, core, y, z_at(e + 1))
                arrived(t, hf, slot)

                @pl.when(middle)
                def _():
                    copy(t, hf, slot, 31 + e, z_next(e)).start()

                copy(t, hf, slot, 4 + e, axis_devs[hf][0]).start()
                copy(t, hf, slot, 8 + e, axis_devs[hf][1]).start()
                copy(t, hf, slot, 16 + e, core_dev).start()

        @pl.when((e >= 3) & (e < 7))
        def _():
            j = e - 3
            zz = z_at(j)
            for hf in range(2):
                slot = near(hf, zz, 1 - (y, x)[hf], (x, y)[hf])
                arrived(t, hf, slot)
                copy(t, hf, slot, 11 + j, axis_devs[hf][1]).start()
                copy(t, hf, slot, 19 + j, core_dev).start()

        @pl.when((e >= 7) & (e < 15))
        def _():
            j = e - 7
            zz = z_at(lax.rem(j, z_size))
            for hf in range(2):
                first = lax.rem((y, x)[hf] + j // z_size, 2)
                slot = near(hf, zz, first, 1 - (x, y)[hf])
                arrived(t, hf, slot)
                copy(t, hf, slot, 23 + j, core_dev).start()

    def small(k, slot, index, target):
        ref = (sbuf, cbuf)[k].at[slot]
        return pltpu.make_async_remote_copy(
            src_ref=ref,
            dst_ref=ref,
            send_sem=small_send.at[k, index],
            recv_sem=small_recv.at[k, slot],
            device_id=target,
            device_id_type=MESH,
        )

    def small_begin(k):
        z_neighbours(lambda i, target: small(k, mp, i, target).start())
        small(k, mp, 2, y_dev).start()

    def small_forward(k):
        for e in range(z_size - 1):
            slot = z_at(e + 1) * 2 + y
            small(k, slot, 0, y_dev).wait_recv()

            @pl.when(middle)
            def _():
                small(k, slot, 6 + e, z_next(e)).start()

            small(k, slot, 3 + e, y_dev).start()

    def small_finish(k):
        for j in range(z_size):
            slot = z_at(j) * 2 + 1 - y
            small(k, slot, 0, y_dev).wait_recv()

    jbuf[me] = jnp.concatenate(
        [joined_ref[...], jnp.zeros((pad_cols - block_cols, depth), jnp.float32)], axis=0
    ).astype(jnp.bfloat16)
    sbuf[mp] = jnp.concatenate(
        [
            step_ref[...].astype(jnp.float32),
            jnp.zeros((STEP_ROWS - requests, step_ref.shape[1]), jnp.float32),
        ],
        axis=0,
    ).astype(jnp.bfloat16)
    pl.semaphore_wait(barrier, 4 + lax.rem((z + 1) // 2, 2))
    small_begin(0)
    begin(0)

    for hh in range(2):
        base = hh * (DN + DV)
        ubuf[me, :, base : base + DN] = up_ref[:, base : base + DN].astype(jnp.bfloat16)
        ubuf[me, :, base + DN : base + DN + DV] = (
            up_ref[:, base + DN : base + DN + DV].T.astype(jnp.bfloat16)
        )
    obuf[me] = out_w_ref[...].astype(jnp.bfloat16)
    cbuf[mp] = cache_ref[...]
    small_forward(0)

    @pl.loop(0, rows // 64)
    def _(i):
        at = pl.ds(pl.multiple_of(i * 64, 64), 64)
        part = rms_scale(x_ref[at, :], gain_ref[...]).astype(jnp.bfloat16)
        for d in range(dp_size):
            normed[d, at, :] = part[:, d * depth : (d + 1) * depth]

    @pl.loop(0, proj.shape[0] // 64)
    def _(i):
        proj[pl.ds(pl.multiple_of(i * 64, 64), 64), :] = jnp.zeros((64, lanes), jnp.float32)

    small_finish(0)
    step_full = jnp.concatenate([sbuf[m] for m in range(mp_size)], axis=1)
    part = rms_scale(step_full, gain_ref[...]).astype(jnp.bfloat16)
    for d in range(dp_size):
        normed[d, rows : rows + STEP_ROWS, :] = part[:, d * depth : (d + 1) * depth]
        normed[d, rows + STEP_ROWS :, :] = jnp.zeros((STEP_LANES - STEP_ROWS, depth), jnp.bfloat16)

    def slot_at(hf, n, cc):
        zz = z_at(n % 4)
        first = lax.rem((y, x)[hf] + n // 4, 2)
        second = lax.rem((x, y)[hf] + n // 8, 2)
        if hf == 0:
            return slot_of(second, cc, first, zz)
        return slot_of(first, cc, second, zz)

    def project(n, cc, wait):
        for hf in range(2):
            slot = slot_at(hf, n, cc)
            if wait:
                arrived(0, hf, slot)
            lo, hi = cuts[0][hf], cuts[0][hf + 1]
            valid = min(hi, block_cols) - lo
            total = mxu(jbuf[slot, lo:hi, :], normed[slot // mp_size], NT)
            at = pl.ds(pl.multiple_of(lax.rem(slot, mp_size) * block_cols + lo, 8), valid)
            proj[at, :] += total[:valid]

    project(0, core, False)

    @pl.loop(1, 16)
    def _(n):
        event(0, n - 1)

        @pl.when(n == 4)
        def _():
            begin(1)
            small_begin(1)

        @pl.when(n == 11)
        def _():
            begin(2)

        @pl.when(n >= 10)
        def _():
            event(1, n - 10)

        project(n, core, False)
        project(n - 1, 1 - core, True)

    @pl.loop(6, 7)
    def _(e):
        event(1, e)

    small_forward(1)
    project(15, 1 - core, True)

    def sibling_arrived(t, m):
        for xx in range(2):
            for hf in range(2):
                arrived(t, hf, (xx * 2 + 1 - core) * mp_size + m)

    lane = lax.broadcasted_iota(jnp.int32, (DR // 2, lanes), 1)
    positions = jnp.where(lane < rows, lane, 0)
    for r in range(requests):
        positions = jnp.where(lane == rows + r, lengths_ref[r], positions)
    step = lax.broadcasted_iota(jnp.int32, (DR // 2, lanes), 0).astype(jnp.float32)
    angles = positions.astype(jnp.float32) * jnp.exp(step * (-2.0 * math.log(ROPE_BASE) / DR))
    cosine_s[...] = jnp.cos(angles)
    sine_s[...] = jnp.sin(angles)

    head_cols = H * (DN + DR)
    latent = proj[head_cols : head_cols + LAT, :].astype(jnp.bfloat16).astype(jnp.float32)
    mean_square = jnp.mean(latent * latent, axis=0, keepdims=True)
    lat_gain = jnp.broadcast_to(lat_gain_ref[...], (8, LAT)).T[:, :1]
    latent = latent * lax.rsqrt(mean_square + NORM_EPS) * lat_gain
    lat_t[...] = latent.astype(jnp.bfloat16)

    def turned(part):
        part = part.astype(jnp.bfloat16).astype(jnp.float32)
        low, high = part[: DR // 2], part[DR // 2 :]
        cosine, sine = cosine_s[...], sine_s[...]
        return jnp.concatenate(
            [low * cosine - high * sine, high * cosine + low * sine], axis=0
        )

    keys[:, :LAT] = latent.T.astype(jnp.bfloat16)
    keys[:, LAT:] = turned(proj[head_cols + LAT : head_cols + LAT + DR, :]).T.astype(jnp.bfloat16)
    q_steps[...] = jnp.zeros_like(q_steps)
    scale2 = (DN + DR) ** (-0.5) * math.log2(math.e)
    half = rows // 2
    causal = lax.broadcasted_iota(jnp.int32, (half, half), 0) <= lax.broadcasted_iota(
        jnp.int32, (half, half), 1
    )

    def attend(scores, values):
        peak = jnp.max(scores, axis=0, keepdims=True)
        weights = jnp.exp2((scores - peak) * scale2)
        weight_sum = jnp.sum(weights, axis=0, keepdims=True)
        summed = mxu(values, weights.astype(jnp.bfloat16))
        return (summed * (1.0 / weight_sum)).astype(jnp.bfloat16)

    def uk_uv(m, hh):
        base = hh * (DN + DV)
        w_uk = jnp.concatenate(
            [ubuf[d * mp_size + m, :, base : base + DN] for d in range(dp_size)], axis=0
        )
        w_uv_t = jnp.concatenate(
            [ubuf[d * mp_size + m, :, base + DN : base + DN + DV] for d in range(dp_size)], axis=1
        )
        return w_uk, w_uv_t

    @pl.loop(0, mp_size)
    def _(k):
        event(1, 7 + k)
        m = z_at(lax.rem(k, z_size)) * 2 + lax.rem(y + k // z_size, 2)
        sibling_arrived(1, m)
        for hh in range(2):
            event(2, 2 * k + hh)
            first = pl.multiple_of(m * 2 * (DN + DR), 2 * (DN + DR)) + hh * (DN + DR)
            first = pl.multiple_of(first, 64)
            w_uk, w_uv_t = uk_uv(m, hh)
            nope = proj[pl.ds(first, DN), :].astype(jnp.bfloat16)
            q_rot = turned(proj[pl.ds(first + DN, DR), :]).astype(jnp.bfloat16)
            q_lat = mxu(w_uk, nope).astype(jnp.bfloat16)
            query = jnp.concatenate([q_lat, q_rot], axis=0)
            q_steps[...] += pltpu.roll(
                query[:, rows:].astype(jnp.float32), m * 8 + hh * 4, axis=1
            )
            scores = mxu(keys[:half, :], query[:, :half])
            low = attend(jnp.where(causal, scores, MASKED), lat_t[:, :half])
            top = mxu(keys[:half, :], query[:, half:rows])
            end = mxu(keys[half:rows, :], query[:, half:rows])
            scores = jnp.concatenate([top, jnp.where(causal, end, MASKED)], axis=0)
            high = attend(scores, lat_t[:, :rows])
            column = pl.ds(pl.multiple_of(m * 2 * DV + hh * DV, DV), DV)
            heads[:half, column] = mxu(w_uv_t, low).T.astype(jnp.bfloat16)
            heads[half:rows, column] = mxu(w_uv_t, high).T.astype(jnp.bfloat16)

    small_finish(1)
    own_keys = keys[rows : rows + STEP_ROWS, :]
    all_keys = jnp.concatenate([cbuf[m] for m in range(mp_size)] + [own_keys], axis=0)
    cached = mp_size * cache_ref.shape[0]
    column = lax.broadcasted_iota(jnp.int32, (8, cached), 1)
    request = lax.rem(lax.broadcasted_iota(jnp.int32, (8, cached), 0), requests)
    slot, entry = column // page_rows, lax.rem(column, page_rows)
    bias = jnp.full((8, cached), MASKED, jnp.float32)
    for r in range(requests):
        for page in range(table_ref.shape[1]):
            counts = (slot == table_ref[r, page]) & (page * page_rows + entry < lengths_ref[r])
            bias = jnp.where(counts & (request == r), 0.0, bias)
    own = lax.broadcasted_iota(jnp.int32, (8, STEP_ROWS), 1) == lax.rem(
        lax.broadcasted_iota(jnp.int32, (8, STEP_ROWS), 0), requests
    )
    bias = jnp.concatenate([bias, jnp.where(own, 0.0, MASKED)], axis=1)
    live = H * requests
    bias = jnp.concatenate([bias] * (live // 8), axis=0)
    scores = mxu(q_steps[...].T[:live].astype(jnp.bfloat16), all_keys, NT) + bias
    peak = jnp.max(scores, axis=1, keepdims=True)
    weights = jnp.exp2((scores - peak) * scale2)
    weight_sum = jnp.sum(weights, axis=1, keepdims=True)
    summed = mxu(weights.astype(jnp.bfloat16), all_keys[:, :LAT])
    step_latent = (summed / weight_sum).astype(jnp.bfloat16)
    heads[rows:, :] = jnp.zeros((STEP_ROWS, H * DV), jnp.bfloat16)
    for h in range(H):
        _, w_uv_t = uk_uv(h // 2, h % 2)
        part = mxu(step_latent, w_uv_t, NT)
        padded = jnp.concatenate(
            [part[4 * h : 4 * h + 4], jnp.zeros((STEP_ROWS - 4, DV), jnp.float32)], axis=0
        )
        heads[rows:, h * DV : (h + 1) * DV] = padded.astype(jnp.bfloat16)

    @pl.loop(0, mp_size)
    def _(m):
        sibling_arrived(2, m)
        total = mxu(heads[:, :depth], obuf[m])
        for d in range(1, dp_size):
            total += mxu(heads[:, d * depth : (d + 1) * depth], obuf[d * mp_size + m])
        width = total.shape[1]
        done = total.astype(jnp.bfloat16)
        out_ref[:, pl.ds(pl.multiple_of(m * width, width), width)] = done[:rows]

        @pl.when(m == mp)
        def _():
            step_out_ref[...] = total[rows : rows + requests].astype(jnp.bfloat16)

    def z_sent(wait, count):
        z_neighbours(lambda i, target: wait(i))

        @pl.when(middle)
        def _():
            for e in range(z_size - 1):
                wait(count + e)

    for t in range(3):
        for hf in range(2):
            sent = lambda i: copy(t, hf, me, i, core_dev).wait_send()
            z_sent(sent, 31)

            @pl.loop(3, 31)
            def _(i):
                sent(i)

    for k in range(2):
        sent = lambda i: small(k, mp, i, y_dev).wait_send()
        z_sent(sent, 6)
        for i in range(2, 6):
            sent(i)


def fused_device(
    prompt_rows,
    step_rows,
    attn_gain,
    latent_gain,
    joined_qkva,
    kv_up,
    out_proj,
    latent_cache,
    page_table,
    cached_lengths,
):
    rows, d_model = prompt_rows.shape
    dp_size, mp_size = lax.axis_size("dp"), lax.axis_size("mp")
    block_cols = joined_qkva.shape[1]
    pad_cols = -(-block_cols // 16) * 16
    requests = step_rows.shape[0]
    slot_count, page_rows, key_width = latent_cache.shape
    lanes = rows + STEP_LANES
    sizes = (rows, dp_size, mp_size, block_cols, mp_size // 2, page_rows)
    devices = dp_size * mp_size
    bf16, f32 = jnp.bfloat16, jnp.float32
    vmem = pl.BlockSpec(memory_space=pltpu.VMEM)
    prompt_out, step_out = pl.pallas_call(
        functools.partial(fused_kernel, sizes),
        out_shape=(
            jax.ShapeDtypeStruct((rows, d_model), bf16),
            jax.ShapeDtypeStruct((requests, out_proj.shape[1]), bf16),
        ),
        in_specs=[vmem] * 8 + [pl.BlockSpec(memory_space=pltpu.SMEM)] * 2,
        out_specs=(vmem, vmem),
        scratch_shapes=[
            pltpu.VMEM((devices, pad_cols, joined_qkva.shape[0]), bf16),
            pltpu.VMEM((devices,) + kv_up.shape, bf16),
            pltpu.VMEM((devices,) + out_proj.shape, bf16),
            pltpu.VMEM((mp_size, STEP_ROWS, step_rows.shape[1]), bf16),
            pltpu.VMEM((mp_size, slot_count * page_rows, key_width), bf16),
            pltpu.VMEM((dp_size, lanes, joined_qkva.shape[0]), bf16),
            pltpu.VMEM((mp_size * block_cols, lanes), f32),
            pltpu.VMEM((LAT, lanes), bf16),
            pltpu.VMEM((lanes, LAT + DR), bf16),
            pltpu.VMEM((LAT + DR, STEP_LANES), f32),
            pltpu.VMEM((rows + STEP_ROWS, H * DV), bf16),
            pltpu.VMEM((DR // 2, lanes), f32),
            pltpu.VMEM((DR // 2, lanes), f32),
            pltpu.SemaphoreType.DMA((3, 2, 34)),
            pltpu.SemaphoreType.DMA((3, 2, devices)),
            pltpu.SemaphoreType.DMA((2, 9)),
            pltpu.SemaphoreType.DMA((2, mp_size)),
        ],
        compiler_params=pltpu.CompilerParams(
            collective_id=0, has_side_effects=True, vmem_limit_bytes=64 * 1024 * 1024
        ),
    )(
        prompt_rows,
        step_rows,
        attn_gain[None, :],
        latent_gain[None, :],
        joined_qkva.T,
        kv_up,
        out_proj,
        latent_cache.reshape(slot_count * page_rows, key_width),
        page_table,
        cached_lengths,
    )
    return prompt_out, step_out


def solution(mesh):
    placed = (
        P(("dp", "mp"), None),
        P("dp", "mp"),
        P(),
        P(),
        P("dp", "mp"),
        P("dp", "mp"),
        P("dp", "mp"),
        P(("dp", "mp"), None, None),
        P("dp", None),
        P("dp"),
    )
    fits = mesh.shape["dp"] == 4 and mesh.shape["mp"] == 8
    return jax.shard_map(
        fused_device if fits else on_device,
        mesh=mesh,
        in_specs=placed,
        out_specs=(P(("dp", "mp"), None), P("dp", "mp")),
        check_vma=False,
    )
```
